32 devices in a mesh: tm: 4 (over y, core), pix: 8 (over z, x).
Axes of the slice: x: 2, y: 2, z: 4, core: 2. Of those that a mesh axis runs over, the one named last changes fastest.
Arguments:
- activations: bfloat16 [4, 20480, 256], P('tm', 'pix'), may hold values from -6 to 6
- down_weight: bfloat16 [1024, 256], replicated, may hold values from -0.1875 to 0.1875
- down_bias: float32 [256], replicated, may hold values from -3 to 3
- taps: float32 [9, 256], replicated, may hold values from -2 to 2
- point_weight: bfloat16 [256, 256], replicated, may hold values from -0.375 to 0.375
- time_mix: float32 [4, 4, 256], replicated, may hold values from -3 to 3
- edge_rows: int32 [8, 2, 20], P('pix'), may hold values from 0 to 19, as said below
- cotangent: bfloat16 [4, 5120, 256], P(None, ('pix', 'tm')), may hold values from -6 to 6
Outputs:
- grad_input: bfloat16 [4, 20480, 256], P('tm', 'pix')
- grad_down: float32 [1024, 256], replicated
- grad_bias: float32 [256], replicated
- grad_taps: float32 [9, 256], replicated
- grad_point: float32 [256, 256], replicated
- grad_mix: float32 [4, 4, 256], replicated
The draws below stay inside these ranges and needn't reach their ends.
Inputs may be any that keep to these rules, and one draw needn't show every extreme that they name: Each edge_rows[t, e] is either 0, 1, .., 19 or its reversal; edge_rows[t, 1] equals edge_rows[(t + 1) mod 8, 0].
All inputs are finite; a program needn't handle non-finite values.
Results may differ from the reference program's by a relative error of at most 0.014.
Values may be sent and summed in bfloat16 or wider, within the bound.
A program may use at most 64 MiB of HBM per device.

```python
import math
import jax
import jax.numpy as jnp
from jax import lax

C = 256
TR = 20
TC = 32
TILES = 8
FRAMES = 4
N8 = 5120
N9 = 20480


def draw_edge_rows(key, part):
    flips = jax.random.randint(key, (TILES,), 0, 2)
    ident = jnp.arange(TR, dtype=jnp.int32)
    backward = TR - 1 - ident
    east_maps = jnp.where(flips[:, None] == 1, backward[None, :], ident[None, :])
    west_maps = jnp.roll(east_maps, 1, axis=0)
    return jnp.stack([west_maps, east_maps], axis=1).astype(jnp.int32)


def block_scale(stream_key, shape, cuts, smallest, top_value):
    def one(dim, blocks):
        draws = jax.random.uniform(jax.random.fold_in(jax.random.fold_in(stream_key, 6), dim), (blocks,), jnp.float32, smallest / len(cuts), top_value / len(cuts))
        return jnp.repeat(jnp.exp(draws), shape[dim] // blocks).reshape((-1,) + (1,) * (len(shape) - dim - 1))

    loudness = one(*cuts[0])
    for cut in cuts[1:]:
        loudness = loudness * one(*cut)
    return loudness


def centred(stream_key, dims, scale, bound, split=(), held_as=jnp.bfloat16):
    gain = block_scale(stream_key, dims, split, -0.22, 0.18) if split else 1.0
    entries = jax.random.normal(stream_key, dims, jnp.float32) * scale * gain
    return jnp.minimum(jnp.maximum(entries, -bound), bound).astype(held_as)


def setup_inputs(seed: int = 0) -> dict:
    seeds = jax.random.split(jax.random.key(seed), 9)
    return {
        "activations": centred(seeds[0], (FRAMES, N9, C), 1.0, 6.0, ((0, 4), (1, 8))),
        "down_weight": centred(seeds[1], (4 * C, C), (4 * C) ** -0.5, 0.1875),
        "down_bias": centred(seeds[2], (C,), 0.5, 3.0, (), jnp.float32),
        "taps": centred(seeds[3], (9, C), 9 ** -0.5, 2.0, (), jnp.float32),
        "point_weight": centred(seeds[4], (C, C), C ** -0.5, 0.375),
        "time_mix": centred(seeds[5], (FRAMES, FRAMES, C), FRAMES ** -0.5, 3.0, (), jnp.float32),
        "edge_rows": draw_edge_rows(jax.random.fold_in(seeds[8], 71), 0),
        "cotangent": centred(seeds[7], (FRAMES, N8, C), 1.0, 6.0, ((1, 32),)),
    }


def depthwise(field, taps, edge_rows):
    west_map = edge_rows[:, 0]
    east_map = edge_rows[:, 1]
    west_col = jnp.roll(field[:, :, :, TC - 1, :], 1, axis=1)
    west_col = jnp.take_along_axis(west_col, jnp.broadcast_to(west_map[None, :, :, None], west_col.shape), axis=2)
    east_col = jnp.roll(field[:, :, :, 0, :], -1, axis=1)
    east_col = jnp.take_along_axis(east_col, jnp.broadcast_to(east_map[None, :, :, None], east_col.shape), axis=2)
    widened = jnp.concatenate([west_col[:, :, :, None, :], field, east_col[:, :, :, None, :]], axis=3)
    widened = jnp.pad(widened, ((0, 0), (0, 0), (1, 1), (0, 0), (0, 0)))
    result = jnp.zeros(field.shape, jnp.float32)
    for row_off in range(3):
        for col_off in range(3):
            result = result + taps[row_off * 3 + col_off] * widened[:, :, row_off:row_off + TR, col_off:col_off + TC, :]
    return result

def reference(activations, down_weight, down_bias, taps, point_weight, time_mix, edge_rows, cotangent):
    total = FRAMES * N8
    rows_in = activations.reshape(total, 4 * C)
    preact = jnp.dot(rows_in, down_weight, preferred_element_type=jnp.float32) + down_bias
    pooled = jax.nn.silu(preact).astype(jnp.bfloat16)
    field = pooled.reshape(FRAMES, TILES, TR, TC, C).astype(jnp.float32)
    spread, pullback = jax.vjp(lambda inner, kern: depthwise(inner, kern, edge_rows), field, taps)
    spread_low = spread.astype(jnp.bfloat16).reshape(total, C)
    mixed_in = (pooled.astype(jnp.float32) + jnp.dot(spread_low, point_weight, preferred_element_type=jnp.float32)).astype(jnp.bfloat16)
    mixed_f = mixed_in.reshape(FRAMES, N8, C).astype(jnp.float32)
    cot_f = cotangent.astype(jnp.float32)
    scale = 1.0 / math.sqrt(FRAMES * N8)
    grad_mix = jnp.einsum('gpc,fpc->fgc', mixed_f, cot_f, precision=lax.Precision.HIGHEST) * scale
    mixed_grad = jnp.einsum('fgc,fpc->gpc', time_mix, cot_f, precision=lax.Precision.HIGHEST).astype(jnp.bfloat16)
    mixed_rows = mixed_grad.reshape(total, C)
    grad_point = jnp.dot(spread_low.T, mixed_rows, preferred_element_type=jnp.float32) * scale
    spread_grad = jnp.dot(mixed_rows, point_weight.T, preferred_element_type=jnp.float32).astype(jnp.bfloat16)
    field_grad, taps_grad = pullback(spread_grad.reshape(FRAMES, TILES, TR, TC, C).astype(jnp.float32))
    pooled_grad = mixed_rows.astype(jnp.float32) + field_grad.reshape(total, C)
    sigma = jax.nn.sigmoid(preact)
    pre_grad = (pooled_grad * (sigma * (1.0 + preact * (1.0 - sigma)))).astype(jnp.bfloat16)
    grad_bias = lax.optimization_barrier(jnp.sum(pre_grad.astype(jnp.float32), axis=0)) * scale
    grad_down = jnp.dot(rows_in.T, pre_grad, preferred_element_type=jnp.float32) * scale
    grad_input = jnp.dot(pre_grad, down_weight.T, preferred_element_type=jnp.float32).astype(jnp.bfloat16)
    return (grad_input.reshape(FRAMES, N9, C), grad_down, grad_bias, taps_grad * scale, grad_point, grad_mix)
```

```python
import functools
import math

import jax
import jax.numpy as jnp
from jax import lax
from jax.experimental import pallas as pl
from jax.experimental.pallas import tpu as pltpu
from jax.sharding import PartitionSpec as P

C = 256
TR = 20
TC = 32
MESH = pl.DeviceIdType.MESH


def padded_2(cells, sides, width):
    for axis, dim in sides:
        count = lax.axis_size(axis)
        head = lax.slice_in_dim(cells, 0, width, axis=dim)
        tail = lax.slice_in_dim(cells, cells.shape[dim] - width, cells.shape[dim], axis=dim)
        cells = jnp.concatenate(
            [
                lax.ppermute(tail, axis, [(i, (i + 1) % count) for i in range(count)]),
                cells,
                lax.ppermute(head, axis, [((i + 1) % count, i) for i in range(count)]),
            ],
            axis=dim,
        )
    return cells


def total_kernel(
    rows, scale, down, point, taps, mix, bias, out_down, out_point, out_taps, out_mix, out_bias,
    packed, core_in, half, parts, mine, gathered, other,
    core_sems, part_send, part_recv, all_send, all_recv, pair_send, pair_recv,
):
    tm, pix = lax.axis_index("tm"), lax.axis_index("pix")
    n_pix = lax.axis_size("pix")
    group = lax.axis_size("tm") // 2 * n_pix
    core = lax.rem(tm, 2)
    me = tm // 2 * n_pix + pix
    partner = (tm + 1 - 2 * core, pix)

    def peer(step):
        index = lax.rem(me + step, group)
        return index, (index // n_pix * 2 + core, lax.rem(index, n_pix))

    barrier = pltpu.get_barrier_semaphore()
    pl.semaphore_signal(barrier, inc=1, device_id=partner, device_id_type=MESH)

    @pl.loop(1, group)
    def _(step):
        _, device = peer(step)
        pl.semaphore_signal(barrier, inc=1, device_id=device, device_id_type=MESH)

    small = jnp.concatenate([taps[...], mix[...], bias[...], jnp.zeros((6, C), jnp.float32)], axis=0)
    for side in range(2):
        lanes = slice(side * 128, side * 128 + 128)
        packed[side, 0:1024, :] = down[:, lanes].astype(jnp.bfloat16)
        packed[side, 1024:1280, :] = point[:, lanes].astype(jnp.bfloat16)
        packed[side, 1280:1312, :] = small[:, lanes].astype(jnp.bfloat16)
        packed[side, 1312:, :] = jnp.zeros((group * rows - 1312, 128), jnp.bfloat16)
    pl.semaphore_wait(barrier, group)

    swap = pltpu.make_async_remote_copy(
        packed.at[1 - core], core_in, core_sems.at[0], core_sems.at[1], partner, MESH
    )
    swap.start()
    swap.wait()
    half[...] = (packed[core].astype(jnp.float32) + core_in[...].astype(jnp.float32)).astype(
        jnp.bfloat16
    )

    def block(ref, index):
        return ref.at[pl.ds(pl.multiple_of(index * rows, 16), rows)]

    def send_part(step):
        index, device = peer(step)
        return pltpu.make_async_remote_copy(
            block(half, index), parts.at[step], part_send.at[step], part_recv.at[step], device, MESH
        )

    @pl.loop(1, group)
    def _(step):
        send_part(step).start()

    parts[0] = half[pl.ds(pl.multiple_of(me * rows, 16), rows), :]

    @pl.loop(1, group)
    def _(step):
        send_part(step).wait()

    def add(step, total):
        return total + parts[step].astype(jnp.float32)

    mine[...] = lax.fori_loop(0, group, add, jnp.zeros((rows, 128), jnp.float32)).astype(
        jnp.bfloat16
    )

    def send_all(step):
        _, device = peer(step)
        return pltpu.make_async_remote_copy(
            mine, gathered.at[step], all_send.at[step], all_recv.at[step], device, MESH
        )

    def send_pair(step):
        return pltpu.make_async_remote_copy(
            gathered.at[step], other.at[step], pair_send.at[step], pair_recv.at[step], partner, MESH
        )

    @pl.loop(1, group)
    def _(step):
        send_all(step).start()

    gathered[0] = mine[...]
    send_pair(0).start()

    @pl.loop(1, group)
    def _(step):
        send_all(step).wait()
        send_pair(step).start()

    @pl.loop(0, group)
    def _(step):
        send_pair(step).wait()

    @pl.loop(0, group)
    def _(step):
        index = lax.rem(me + group - step, group)
        place = pl.ds(pl.multiple_of(index * rows, 16), rows)
        packed[core, place, :] = gathered[step]
        packed[1 - core, place, :] = other[step]

    for side in range(2):
        lanes = slice(side * 128, side * 128 + 128)
        out_down[:, lanes] = packed[side, 0:1024, :].astype(jnp.float32) * scale
        out_point[:, lanes] = packed[side, 1024:1280, :].astype(jnp.float32) * scale
        tail = packed[side, 1280:1312, :].astype(jnp.float32) * scale
        out_taps[:, lanes] = tail[0:9]
        out_mix[:, lanes] = tail[9:25]
        out_bias[:, lanes] = tail[25:26]


def total_over_devices(down, point, taps, mix, bias, scale):
    group = lax.axis_size("tm") // 2 * lax.axis_size("pix")
    rows = -(-1312 // (16 * group)) * 16
    low = jnp.bfloat16
    sems = pltpu.SemaphoreType.DMA((group,))
    outs = [jax.ShapeDtypeStruct(x.shape, jnp.float32) for x in (down, point, taps, mix, bias)]
    return pl.pallas_call(
        functools.partial(total_kernel, rows, scale),
        out_shape=outs,
        in_specs=[pl.BlockSpec(memory_space=pltpu.VMEM)] * 5,
        out_specs=[pl.BlockSpec(memory_space=pltpu.VMEM)] * 5,
        scratch_shapes=[
            pltpu.VMEM((2, group * rows, 128), low),
            pltpu.VMEM((group * rows, 128), low),
            pltpu.VMEM((group * rows, 128), low),
            pltpu.VMEM((group, rows, 128), low),
            pltpu.VMEM((rows, 128), low),
            pltpu.VMEM((group, rows, 128), low),
            pltpu.VMEM((group, rows, 128), low),
            pltpu.SemaphoreType.DMA((2,)),
            sems, sems, sems, sems, sems, sems,
        ],
        compiler_params=pltpu.CompilerParams(
            collective_id=0, has_side_effects=True, vmem_limit_bytes=40 * 1024 * 1024
        ),
    )(down, point, taps, mix, bias)


def on_device(
    activations, down_weight, down_bias, taps, point_weight, time_mix, edge_rows, cotangent
):
    frames = lax.axis_size("tm")
    tiles = lax.axis_size("pix")
    pixels = TR * TC
    scale = 1.0 / math.sqrt(frames * tiles * pixels)
    rows_in = activations.reshape(pixels, 4 * C)
    preact = jnp.dot(rows_in, down_weight, preferred_element_type=jnp.float32) + down_bias
    pooled = jax.nn.silu(preact).astype(jnp.bfloat16)
    tile_grid = pooled.reshape(1, TR, TC, C)
    padded = padded_2(tile_grid, (("pix", 2),), 1)
    west_map = edge_rows[0, 0]
    east_map = edge_rows[0, 1]
    west_col = jnp.take(padded[0, :, 0, :], west_map, axis=0)
    east_col = jnp.take(padded[0, :, TC + 1, :], east_map, axis=0)
    widened = jnp.concatenate([west_col[:, None, :], tile_grid[0], east_col[:, None, :]], axis=1)
    widened = jnp.pad(widened, ((1, 1), (0, 0), (0, 0)))
    spread = jnp.zeros((TR, TC, C), jnp.float32)
    for row_off in range(3):
        for col_off in range(3):
            spread = (
                spread
                + taps[row_off * 3 + col_off]
                * widened[row_off : row_off + TR, col_off : col_off + TC, :]
            )
    spread_low = spread.astype(jnp.bfloat16).reshape(pixels, C)
    mixed_in = (
        pooled.astype(jnp.float32)
        + jnp.dot(spread_low, point_weight, preferred_element_type=jnp.float32)
    ).astype(jnp.bfloat16)
    by_pixel = lax.all_to_all(
        mixed_in.reshape(1, pixels, C), "tm", split_axis=1, concat_axis=0, tiled=True
    )
    mix_part = jnp.einsum("gpc,fpc->fgc", by_pixel, cotangent, preferred_element_type=jnp.float32)
    cot_f = cotangent.astype(jnp.float32)
    mixed_acc = jnp.zeros((frames, cotangent.shape[1], C), jnp.float32)
    for source in range(frames):
        mixed_acc = mixed_acc + time_mix[source][:, None, :] * cot_f[source][None, :, :]
    mixed_grad = mixed_acc.astype(jnp.bfloat16)
    back_grad = lax.all_to_all(mixed_grad, "tm", split_axis=0, concat_axis=1, tiled=True)
    mixed_rows = back_grad.reshape(pixels, C)
    point_part = jnp.dot(spread_low.T, mixed_rows, preferred_element_type=jnp.float32)
    spread_grad = jnp.dot(mixed_rows, point_weight.T, preferred_element_type=jnp.float32).astype(
        jnp.bfloat16
    )
    grad_float = spread_grad.reshape(TR, TC, C).astype(jnp.float32)
    taps_rows = []
    for row_off in range(3):
        for col_off in range(3):
            taps_rows.append(
                jnp.sum(
                    grad_float * widened[row_off : row_off + TR, col_off : col_off + TC, :],
                    axis=(0, 1),
                )
            )
    taps_part = jnp.stack(taps_rows, axis=0)
    grad_padded = jnp.pad(grad_float, ((2, 2), (2, 2), (0, 0)))
    wide_grad = jnp.zeros((TR + 2, TC + 2, C), jnp.float32)
    for row_off in range(3):
        for col_off in range(3):
            wide_grad = (
                wide_grad
                + taps[row_off * 3 + col_off]
                * grad_padded[2 - row_off : 4 - row_off + TR, 2 - col_off : 4 - col_off + TC, :]
            )
    west_back = jnp.take(wide_grad[1 : TR + 1, 0, :], west_map, axis=0)
    east_back = jnp.take(wide_grad[1 : TR + 1, TC + 1, :], east_map, axis=0)
    outgoing = jnp.stack([west_back, east_back], axis=1)
    incoming = padded_2(outgoing.astype(jnp.bfloat16), (("pix", 1),), 1).astype(outgoing.dtype)
    inner_grad = wide_grad[1 : TR + 1, 1 : TC + 1, :]
    inner_grad = inner_grad.at[:, 0, :].add(incoming[:, 0, :])
    inner_grad = inner_grad.at[:, TC - 1, :].add(incoming[:, 3, :])
    pooled_grad = mixed_rows.astype(jnp.float32) + inner_grad.reshape(pixels, C)
    sigma = jax.nn.sigmoid(preact)
    pre_grad = (pooled_grad * (sigma * (1.0 + preact * (1.0 - sigma)))).astype(jnp.bfloat16)
    bias_part = jnp.sum(pre_grad.astype(jnp.float32), axis=0)
    down_part = jnp.dot(rows_in.T, pre_grad, preferred_element_type=jnp.float32)
    grad_input = jnp.dot(pre_grad, down_weight.T, preferred_element_type=jnp.float32).astype(
        jnp.bfloat16
    )
    totals = total_over_devices(
        down_part,
        point_part,
        taps_part,
        mix_part.reshape(frames * frames, C),
        bias_part.reshape(1, C),
        scale,
    )
    grad_down, grad_point, grad_taps, grad_mix, grad_bias = totals
    grad_mix = grad_mix.reshape(frames, frames, C)
    grad_bias = grad_bias.reshape(C)
    return (
        grad_input.reshape(1, 4 * pixels, C),
        grad_down,
        grad_bias,
        grad_taps,
        grad_point,
        grad_mix,
    )


def solution(mesh):
    in_specs = (
        P("tm", "pix", None),
        P(),
        P(),
        P(),
        P(),
        P(),
        P("pix", None, None),
        P(None, ("pix", "tm"), None),
    )
    out_specs = (P("tm", "pix", None), P(), P(), P(), P(), P())
    return jax.shard_map(
        on_device, mesh=mesh, in_specs=in_specs, out_specs=out_specs, check_vma=False
    )
```

```python
import functools
import math

import jax
import jax.numpy as jnp
from jax import lax
from jax.experimental import pallas as pl
from jax.experimental.pallas import tpu as pltpu
from jax.sharding import PartitionSpec as P

C = 256
TR = 20
TC = 32
MESH = pl.DeviceIdType.MESH


def kernel(
    rows, scale, act, weight, bias, taps, point, mix, perm, cot,
    out_input, out_down, out_bias, out_taps, out_point, out_mix,
    fine, rows_in, rows_t, preact, pooled, wide, gwide, grad, spread, mixed_low,
    mg_send, mg_recv, mix_send, mix_recv, edge, edge_send, edge_recv, back_send, back_recv, pre,
    packed, core_in, half, parts, mine, gathered, other,
    mg_sems, mix_sems, edge_sems, back_sems,
    core_sems, part_send, part_recv, all_send, all_recv, pair_send, pair_recv,
):
    f32, low = jnp.float32, jnp.bfloat16
    tm, pix = lax.axis_index("tm"), lax.axis_index("pix")
    n_tm, n_pix = lax.axis_size("tm"), lax.axis_size("pix")
    group = n_tm // 2 * n_pix
    core = lax.rem(tm, 2)
    me = tm // 2 * n_pix + pix
    partner = (tm + 1 - 2 * core, pix)
    west, east = (tm, lax.rem(pix + n_pix - 1, n_pix)), (tm, lax.rem(pix + 1, n_pix))
    quarter = TR * TC // n_tm

    def peer(step):
        index = lax.rem(me + step, group)
        return index, (index // n_pix * 2 + core, lax.rem(index, n_pix))

    barrier = pltpu.get_barrier_semaphore()
    pl.semaphore_signal(barrier, inc=1, device_id=partner, device_id_type=MESH)
    across = (lax.rem(partner[0] + 2, n_tm), pix)
    pl.semaphore_signal(barrier, inc=1, device_id=across, device_id_type=MESH)

    @pl.loop(1, group)
    def _(step):
        _, device = peer(step)
        pl.semaphore_signal(barrier, inc=1, device_id=device, device_id_type=MESH)

    for frame in range(n_tm):
        total = mix[frame : frame + 1] * cot[0].astype(f32)
        for source in range(1, n_tm):
            total = total + mix[n_tm * source + frame : n_tm * source + frame + 1] * cot[
                source
            ].astype(f32)
        mg_send[frame] = total.astype(low)
    pl.semaphore_wait(barrier, group + 1)

    def exchange(send, recv, sems, step):
        target = lax.rem(tm + step, n_tm)
        return pltpu.make_async_remote_copy(
            send.at[target], recv.at[tm], sems.at[0, step], sems.at[1, step], (target, pix), MESH
        )

    for step in range(1, n_tm):
        exchange(mg_send, mg_recv, mg_sems, step).start()
    mg_recv[tm] = mg_send[tm]

    @pl.loop(0, 2560 // 160)
    def _(i):
        at = pl.ds(pl.multiple_of(i * 160, 160), 160)
        for side in range(2):
            fine[side, at, :] = act[at, side * 128 : side * 128 + 128].astype(f32)

    for child in range(4):
        for side in range(2):
            lanes = slice(child * C + side * 128, child * C + side * 128 + 128)
            rows_in[:, lanes] = fine[side, pl.ds(child, TR * TC, stride=4), :].astype(low)

    @pl.loop(0, 4)
    def _(i):
        at = pl.ds(pl.multiple_of(i * 160, 160), 160)
        value = jnp.dot(rows_in[at, :], weight[...], preferred_element_type=f32) + bias[...]
        preact[at, :] = value
        pooled[at, :] = (value / (1.0 + jnp.exp(-value))).astype(low)

    def shifted(ref, values, r):
        ref[1, r + 1] = values
        ref[0, r + 1, 1:TC, :] = values[0 : TC - 1]
        ref[2, r + 1, 0 : TC - 1, :] = values[1:TC]

    for side in range(3):
        for r in (0, TR + 1):
            wide[side, r] = jnp.zeros((TC, C), f32)
            gwide[side, r] = jnp.zeros((TC, C), f32)

    @pl.loop(0, TR)
    def _(r):
        shifted(wide, pooled[pl.ds(pl.multiple_of(r * TC, TC), TC), :].astype(f32), r)

    edge[...] = jnp.zeros(edge.shape, f32)
    for r in range(TR):
        edge[0, r : r + 1] = wide[1, r + 1, 0:1, :]
        edge[1, r : r + 1] = wide[1, r + 1, TC - 1 : TC, :]
    edge_send[...] = edge[...].astype(low)

    def swap_edges(send, recv, sems):
        return [
            pltpu.make_async_remote_copy(
                send.at[0], recv.at[1], sems.at[0, 0], sems.at[1, 0], west, MESH
            ),
            pltpu.make_async_remote_copy(
                send.at[1], recv.at[0], sems.at[0, 1], sems.at[1, 1], east, MESH
            ),
        ]

    forward = swap_edges(edge_send, edge_recv, edge_sems)
    for copy in forward:
        copy.start()

    for child in range(4):
        lanes = slice(child * C, child * C + C)
        rows_t[lanes, :] = rows_in[:, lanes].T

    for step in range(1, n_tm):
        exchange(mg_send, mg_recv, mg_sems, step).wait()

    @pl.loop(0, n_tm)
    def _(i):
        value = lax.dot_general(
            mg_recv[i], point[...], (((1,), (1,)), ((), ())), preferred_element_type=f32
        )
        pre[pl.ds(pl.multiple_of(i * quarter, quarter), quarter), :] = value.astype(low)

    @pl.loop(0, TR)
    def _(r):
        shifted(gwide, pre[pl.ds(pl.multiple_of(r * TC, TC), TC), :].astype(f32), r)
        gwide[0, r + 1, 0:1, :] = jnp.zeros((1, C), f32)
        gwide[2, r + 1, TC - 1 : TC, :] = jnp.zeros((1, C), f32)

    edge[...] = jnp.zeros(edge.shape, f32)
    for r in range(TR):
        edge[0, r + 1 : r + 2] = gwide[1, r + 1, 0:1, :]
        edge[1, r + 1 : r + 2] = gwide[1, r + 1, TC - 1 : TC, :]
    for side in range(2):
        total = jnp.zeros((TR, C), f32)
        for a in range(3):
            tap = 3 * a + 2 * side
            total = total + taps[tap : tap + 1] * edge[side, 2 - a : 2 - a + TR]
        total = jnp.concatenate([total, jnp.zeros((32 - TR, C), f32)], axis=0).astype(low)
        back_send[side] = jnp.dot(perm[side], total, preferred_element_type=f32).astype(low)
    backward = swap_edges(back_send, back_recv, back_sems)
    for copy in backward:
        copy.start()

    for copy in forward:
        copy.wait()
    for side in range(2):
        edge[side] = jnp.dot(perm[side], edge_recv[side], preferred_element_type=f32)
    for r in range(TR):
        wide[0, r + 1, 0:1, :] = edge[0, r : r + 1]
        wide[2, r + 1, TC - 1 : TC, :] = edge[1, r : r + 1]

    def conv(r, sums):
        total = jnp.zeros((TC, C), f32)
        inner = mg_recv[r // (TR // n_tm), pl.ds(
            pl.multiple_of(lax.rem(r, TR // n_tm) * TC, TC), TC
        ), :].astype(f32)
        here = gwide[1, r + 1]
        new = []
        for a in range(3):
            for b in range(3):
                tap = taps[3 * a + b : 3 * a + b + 1]
                cells = wide[b, r + a]
                total = total + tap * cells
                inner = inner + tap * gwide[2 - b, r + 2 - a]
                product = here * cells
                new.append(
                    sums[3 * a + b]
                    + ((product[0:8] + product[8:16]) + (product[16:24] + product[24:32]))
                )
        at = pl.ds(pl.multiple_of(r * TC, TC), TC)
        spread[at, :] = total.astype(low)
        grad[at, :] = inner
        return tuple(new)

    sums = lax.fori_loop(0, TR, conv, tuple(jnp.zeros((8, C), f32) for _ in range(9)))
    taps_part = [jnp.sum(x, axis=0, keepdims=True) for x in sums]

    @pl.loop(0, n_tm)
    def _(i):
        at = pl.ds(pl.multiple_of(i * quarter, quarter), quarter)
        value = jnp.dot(spread[at, :], point[...], preferred_element_type=f32)
        mix_send[i] = (pooled[at, :].astype(f32) + value).astype(low)
        mixed_low[at, :] = mg_recv[i]

    for step in range(1, n_tm):
        exchange(mix_send, mix_recv, mix_sems, step).start()
    mix_recv[tm] = mix_send[tm]

    def pack(first, value):
        for side in range(2):
            packed[side, first : first + value.shape[0], :] = value[
                :, side * 128 : side * 128 + 128
            ].astype(low)

    across_rows = (((0,), (0,)), ((), ()))
    pack(4 * C, lax.dot_general(spread[...], mixed_low[...], across_rows, preferred_element_type=f32))

    for copy in backward:
        copy.wait()
    edge[...] = back_recv[...].astype(f32)
    for r in range(TR):
        grad[r * TC : r * TC + 1, :] += edge[0, r : r + 1]
        grad[r * TC + TC - 1 : r * TC + TC, :] += edge[1, r : r + 1]

    def through(r, total):
        at = pl.ds(pl.multiple_of(r * TC, TC), TC)
        value = preact[at, :]
        sigma = 1.0 / (1.0 + jnp.exp(-value))
        low_grad = (grad[at, :] * (sigma * (1.0 + value * (1.0 - sigma)))).astype(low)
        pre[at, :] = low_grad
        wider = low_grad.astype(f32)
        return total + ((wider[0:8] + wider[8:16]) + (wider[16:24] + wider[24:32]))

    bias_part = lax.fori_loop(0, TR, through, jnp.zeros((8, C), f32))
    for child in range(4):
        lanes = slice(child * C, child * C + C)
        pack(child * C, jnp.dot(rows_t[lanes, :], pre[...], preferred_element_type=f32))

    for step in range(1, n_tm):
        exchange(mix_send, mix_recv, mix_sems, step).wait()

    def mixing(i, sums):
        at = pl.ds(pl.multiple_of(i * 16, 16), 16)
        cots = [cot[f, at, :].astype(f32) for f in range(n_tm)]
        mixes = [mix_recv[g, at, :].astype(f32) for g in range(n_tm)]
        new = []
        for f in range(n_tm):
            for g in range(n_tm):
                product = cots[f] * mixes[g]
                new.append(sums[n_tm * f + g] + (product[0:8] + product[8:16]))
        return tuple(new)

    sums = lax.fori_loop(
        0, quarter // 16, mixing, tuple(jnp.zeros((8, C), f32) for _ in range(n_tm * n_tm))
    )
    small = taps_part + [jnp.sum(x, axis=0, keepdims=True) for x in sums]
    small.append(jnp.sum(bias_part, axis=0, keepdims=True))
    small.append(jnp.zeros((6, C), f32))
    pack(5 * C, jnp.concatenate(small, axis=0))
    for side in range(2):
        packed[side, 1312:, :] = jnp.zeros((group * rows - 1312, 128), low)

    swap = pltpu.make_async_remote_copy(
        packed.at[1 - core], core_in, core_sems.at[0], core_sems.at[1], partner, MESH
    )
    swap.start()
    swap.wait()
    half[...] = (packed[core].astype(f32) + core_in[...].astype(f32)).astype(low)

    def send_part(step):
        index, device = peer(step)
        return pltpu.make_async_remote_copy(
            half.at[pl.ds(pl.multiple_of(index * rows, 16), rows)],
            parts.at[step], part_send.at[step], part_recv.at[step], device, MESH
        )

    @pl.loop(1, group)
    def _(step):
        send_part(step).start()

    parts[0] = half[pl.ds(pl.multiple_of(me * rows, 16), rows), :]

    for child in range(4):
        lanes = slice(child * C, child * C + C)
        value = lax.dot_general(
            pre[...], weight[lanes, :], (((1,), (1,)), ((), ())), preferred_element_type=f32
        )
        for side in range(2):
            fine[side, pl.ds(child, TR * TC, stride=4), :] = value[:, side * 128 : side * 128 + 128]

    @pl.loop(0, 2560 // 160)
    def _(i):
        at = pl.ds(pl.multiple_of(i * 160, 160), 160)
        for side in range(2):
            out_input[at, side * 128 : side * 128 + 128] = fine[side, at, :].astype(low)

    @pl.loop(1, group)
    def _(step):
        send_part(step).wait()

    def add(step, total):
        return total + parts[step].astype(f32)

    mine[...] = lax.fori_loop(0, group, add, jnp.zeros((rows, 128), f32)).astype(low)

    def send_all(step):
        _, device = peer(step)
        return pltpu.make_async_remote_copy(
            mine, gathered.at[step], all_send.at[step], all_recv.at[step], device, MESH
        )

    def send_pair(step):
        return pltpu.make_async_remote_copy(
            gathered.at[step], other.at[step], pair_send.at[step], pair_recv.at[step], partner, MESH
        )

    @pl.loop(1, group)
    def _(step):
        send_all(step).start()

    gathered[0] = mine[...]
    send_pair(0).start()

    @pl.loop(1, group)
    def _(step):
        send_all(step).wait()
        send_pair(step).start()

    @pl.loop(0, group)
    def _(step):
        send_pair(step).wait()

    @pl.loop(0, group)
    def _(step):
        index = lax.rem(me + group - step, group)
        place = pl.ds(pl.multiple_of(index * rows, 16), rows)
        packed[core, place, :] = gathered[step]
        packed[1 - core, place, :] = other[step]

    for side in range(2):
        lanes = slice(side * 128, side * 128 + 128)
        out_down[:, lanes] = packed[side, 0:1024, :].astype(f32) * scale
        out_point[:, lanes] = packed[side, 1024:1280, :].astype(f32) * scale
        tail = packed[side, 1280:1312, :].astype(f32) * scale
        out_taps[:, lanes] = tail[0:9]
        out_mix[:, lanes] = tail[9:25]
        out_bias[:, lanes] = tail[25:26]


def on_device(
    activations, down_weight, down_bias, taps, point_weight, time_mix, edge_rows, cotangent
):
    frames = lax.axis_size("tm")
    tiles = lax.axis_size("pix")
    pixels = TR * TC
    quarter = pixels // frames
    scale = 1.0 / math.sqrt(frames * tiles * pixels)
    group = frames // 2 * tiles
    rows = -(-1312 // (16 * group)) * 16
    f32, low = jnp.float32, jnp.bfloat16
    sems = pltpu.SemaphoreType.DMA((group,))
    both = lambda n: pltpu.SemaphoreType.DMA((2, n))
    place = lax.broadcasted_iota(jnp.int32, (2, 32, 32), 2)
    maps = jnp.pad(edge_rows[0], ((0, 0), (0, 32 - TR)), constant_values=-1)
    perm = (maps[:, :, None] == place).astype(low)
    vmem = pl.BlockSpec(memory_space=pltpu.VMEM)
    outs = pl.pallas_call(
        functools.partial(kernel, rows, scale),
        out_shape=[
            jax.ShapeDtypeStruct((4 * pixels, C), low),
            jax.ShapeDtypeStruct((4 * C, C), f32),
            jax.ShapeDtypeStruct((1, C), f32),
            jax.ShapeDtypeStruct((9, C), f32),
            jax.ShapeDtypeStruct((C, C), f32),
            jax.ShapeDtypeStruct((frames * frames, C), f32),
        ],
        in_specs=[vmem] * 8,
        out_specs=[vmem] * 6,
        scratch_shapes=[
            pltpu.VMEM((2, 4 * pixels, 128), f32),
            pltpu.VMEM((pixels, 4 * C), low),
            pltpu.VMEM((4 * C, pixels), low),
            pltpu.VMEM((pixels, C), f32),
            pltpu.VMEM((pixels, C), low),
            pltpu.VMEM((3, TR + 2, TC, C), f32),
            pltpu.VMEM((3, TR + 2, TC, C), f32),
            pltpu.VMEM((pixels, C), f32),
            pltpu.VMEM((pixels, C), low),
            pltpu.VMEM((pixels, C), low),
            pltpu.VMEM((frames, quarter, C), low),
            pltpu.VMEM((frames, quarter, C), low),
            pltpu.VMEM((frames, quarter, C), low),
            pltpu.VMEM((frames, quarter, C), low),
            pltpu.VMEM((2, 32, C), f32),
            pltpu.VMEM((2, 32, C), low),
            pltpu.VMEM((2, 32, C), low),
            pltpu.VMEM((2, 32, C), low),
            pltpu.VMEM((2, 32, C), low),
            pltpu.VMEM((pixels, C), low),
            pltpu.VMEM((2, group * rows, 128), low),
            pltpu.VMEM((group * rows, 128), low),
            pltpu.VMEM((group * rows, 128), low),
            pltpu.VMEM((group, rows, 128), low),
            pltpu.VMEM((rows, 128), low),
            pltpu.VMEM((group, rows, 128), low),
            pltpu.VMEM((group, rows, 128), low),
            both(frames), both(frames), both(2), both(2),
            pltpu.SemaphoreType.DMA((2,)),
            sems, sems, sems, sems, sems, sems,
        ],
        compiler_params=pltpu.CompilerParams(
            collective_id=0, has_side_effects=True, vmem_limit_bytes=48 * 1024 * 1024
        ),
    )(
        activations.reshape(4 * pixels, C),
        down_weight,
        down_bias.reshape(1, C),
        taps,
        point_weight,
        time_mix.reshape(frames * frames, C),
        perm,
        cotangent,
    )
    return (
        outs[0].reshape(1, 4 * pixels, C),
        outs[1],
        outs[2].reshape(C),
        outs[3],
        outs[4],
        outs[5].reshape(frames, frames, C),
    )


def solution(mesh):
    in_specs = (
        P("tm", "pix", None),
        P(),
        P(),
        P(),
        P(),
        P(),
        P("pix", None, None),
        P(None, ("pix", "tm"), None),
    )
    out_specs = (P("tm", "pix", None), P(), P(), P(), P(), P())
    return jax.shard_map(
        on_device, mesh=mesh, in_specs=in_specs, out_specs=out_specs, check_vma=False
    )
```

```python
import functools
import math

import jax
import jax.numpy as jnp
from jax import lax
from jax.experimental import pallas as pl
from jax.experimental.pallas import tpu as pltpu
from jax.sharding import PartitionSpec as P

C = 256
TR = 20
TC = 32
MESH = pl.DeviceIdType.MESH


def kernel(
    rows, act_in, weight_in, bias_in, taps_in, point_in, mix_in, maps_in, cot_in,
    out_input, out_full,
    act, weight, bias, taps, point, mix, maps, cot, perm, result,
    fine, rows_in, rows_t, preact, pooled, wide, gwide, grad, spread, mixed_low,
    mg_send, mg_recv, mix_send, mix_recv, edge, edge_send, edge_recv, back_send, back_recv, pre,
    packed, core_in, half, plane_in, line_out, line_in, full,
    in_sems, out_sems, mg_sems, mix_sems, edge_sems, back_sems,
    core_sems, plane_sems, line_sems, line_back, plane_send, plane_recv, pair_send, pair_recv,
):
    f32, low = jnp.float32, jnp.bfloat16
    tm, pix = lax.axis_index("tm"), lax.axis_index("pix")
    n_tm, n_pix = lax.axis_size("tm"), lax.axis_size("pix")
    group = n_tm // 2 * n_pix
    core = lax.rem(tm, 2)
    me = tm // 2 * n_pix + pix
    n_plane, n_line = n_tm // 2 * 2, n_pix // 2
    mine, line = tm // 2 * 2 + lax.rem(pix, 2), pix // 2
    partner = (tm + 1 - 2 * core, pix)
    west, east = (tm, lax.rem(pix + n_pix - 1, n_pix)), (tm, lax.rem(pix + 1, n_pix))
    quarter = TR * TC // n_tm

    def peer(step):
        index = lax.rem(me + step, group)
        return index, (index // n_pix * 2 + core, lax.rem(index, n_pix))

    loads = [
        pltpu.make_async_copy(there, here, in_sems.at[i])
        for i, (there, here) in enumerate(
            [
                (cot_in, cot), (mix_in, mix), (act_in, act), (weight_in, weight), (bias_in, bias),
                (point_in, point), (taps_in, taps), (maps_in, maps),
            ]
        )
    ]
    for load in loads:
        load.start()

    barrier = pltpu.get_barrier_semaphore()
    pl.semaphore_signal(barrier, inc=1, device_id=partner, device_id_type=MESH)
    across = (lax.rem(partner[0] + 2, n_tm), pix)
    pl.semaphore_signal(barrier, inc=1, device_id=across, device_id_type=MESH)

    @pl.loop(1, group)
    def _(step):
        _, device = peer(step)
        pl.semaphore_signal(barrier, inc=1, device_id=device, device_id_type=MESH)

    loads[0].wait()
    loads[1].wait()
    for frame in range(n_tm):
        total = mix[0, frame : frame + 1] * cot[0].astype(f32)
        for source in range(1, n_tm):
            total = total + mix[source, frame : frame + 1] * cot[source].astype(f32)
        mg_send[frame] = total.astype(low)
    pl.semaphore_wait(barrier, group + 1)

    def exchange(send, recv, sems, step):
        target = lax.rem(tm + step, n_tm)
        return pltpu.make_async_remote_copy(
            send.at[target], recv.at[tm], sems.at[0, step], sems.at[1, step], (target, pix), MESH
        )

    for step in range(1, n_tm):
        exchange(mg_send, mg_recv, mg_sems, step).start()
    mg_recv[tm] = mg_send[tm]

    for load in loads[2:]:
        load.wait()
    perm[...] = jnp.zeros(perm.shape, f32)
    for side in range(2):
        row = lax.broadcasted_iota(jnp.int32, (TR, TR), 0)
        perm[side, 0:TR, 0:TR] = jnp.where(maps[0, side : side + 1, :] == row, 1.0, 0.0)

    @pl.loop(0, 2560 // 160)
    def _(i):
        at = pl.ds(pl.multiple_of(i * 160, 160), 160)
        for side in range(2):
            fine[side, at, :] = act[at, side * 128 : side * 128 + 128].astype(f32)

    for child in range(4):
        for side in range(2):
            lanes = slice(child * C + side * 128, child * C + side * 128 + 128)
            rows_in[:, lanes] = fine[side, pl.ds(child, TR * TC, stride=4), :].astype(low)

    @pl.loop(0, 4)
    def _(i):
        at = pl.ds(pl.multiple_of(i * 160, 160), 160)
        value = jnp.dot(rows_in[at, :], weight[...], preferred_element_type=f32) + bias[...]
        preact[at, :] = value
        pooled[at, :] = (value / (1.0 + jnp.exp(-value))).astype(low)

    def shifted(ref, values, r):
        ref[1, r + 1] = values
        ref[0, r + 1, 1:TC, :] = values[0 : TC - 1]
        ref[2, r + 1, 0 : TC - 1, :] = values[1:TC]

    for side in range(3):
        for r in (0, TR + 1):
            wide[side, r] = jnp.zeros((TC, C), f32)
            gwide[side, r] = jnp.zeros((TC, C), f32)

    @pl.loop(0, TR)
    def _(r):
        shifted(wide, pooled[pl.ds(pl.multiple_of(r * TC, TC), TC), :].astype(f32), r)

    edge[...] = jnp.zeros(edge.shape, f32)
    for r in range(TR):
        edge[0, r : r + 1] = wide[1, r + 1, 0:1, :]
        edge[1, r : r + 1] = wide[1, r + 1, TC - 1 : TC, :]
    edge_send[...] = edge[...].astype(low)

    def swap_edges(send, recv, sems):
        return [
            pltpu.make_async_remote_copy(
                send.at[0], recv.at[1], sems.at[0, 0], sems.at[1, 0], west, MESH
            ),
            pltpu.make_async_remote_copy(
                send.at[1], recv.at[0], sems.at[0, 1], sems.at[1, 1], east, MESH
            ),
        ]

    forward = swap_edges(edge_send, edge_recv, edge_sems)
    for copy in forward:
        copy.start()

    for child in range(4):
        lanes = slice(child * C, child * C + C)
        rows_t[lanes, :] = rows_in[:, lanes].T

    for step in range(1, n_tm):
        exchange(mg_send, mg_recv, mg_sems, step).wait()

    @pl.loop(0, n_tm)
    def _(i):
        value = lax.dot_general(
            mg_recv[i], point[...], (((1,), (1,)), ((), ())), preferred_element_type=f32
        )
        pre[pl.ds(pl.multiple_of(i * quarter, quarter), quarter), :] = value.astype(low)

    @pl.loop(0, TR)
    def _(r):
        shifted(gwide, pre[pl.ds(pl.multiple_of(r * TC, TC), TC), :].astype(f32), r)
        gwide[0, r + 1, 0:1, :] = jnp.zeros((1, C), f32)
        gwide[2, r + 1, TC - 1 : TC, :] = jnp.zeros((1, C), f32)

    edge[...] = jnp.zeros(edge.shape, f32)
    for r in range(TR):
        edge[0, r + 1 : r + 2] = gwide[1, r + 1, 0:1, :]
        edge[1, r + 1 : r + 2] = gwide[1, r + 1, TC - 1 : TC, :]
    for side in range(2):
        total = jnp.zeros((TR, C), f32)
        for a in range(3):
            tap = 3 * a + 2 * side
            total = total + taps[tap : tap + 1] * edge[side, 2 - a : 2 - a + TR]
        total = jnp.concatenate([total, jnp.zeros((32 - TR, C), f32)], axis=0).astype(low)
        back_send[side] = jnp.dot(perm[side].astype(low), total, preferred_element_type=f32).astype(low)
    backward = swap_edges(back_send, back_recv, back_sems)
    for copy in backward:
        copy.start()

    for copy in forward:
        copy.wait()
    for side in range(2):
        edge[side] = jnp.dot(perm[side].astype(low), edge_recv[side], preferred_element_type=f32)
    for r in range(TR):
        wide[0, r + 1, 0:1, :] = edge[0, r : r + 1]
        wide[2, r + 1, TC - 1 : TC, :] = edge[1, r : r + 1]

    def conv(r, sums):
        total = jnp.zeros((TC, C), f32)
        inner = mg_recv[r // (TR // n_tm), pl.ds(
            pl.multiple_of(lax.rem(r, TR // n_tm) * TC, TC), TC
        ), :].astype(f32)
        here = gwide[1, r + 1]
        new = []
        for a in range(3):
            for b in range(3):
                tap = taps[3 * a + b : 3 * a + b + 1]
                cells = wide[b, r + a]
                total = total + tap * cells
                inner = inner + tap * gwide[2 - b, r + 2 - a]
                product = here * cells
                new.append(
                    sums[3 * a + b]
                    + ((product[0:8] + product[8:16]) + (product[16:24] + product[24:32]))
                )
        at = pl.ds(pl.multiple_of(r * TC, TC), TC)
        spread[at, :] = total.astype(low)
        grad[at, :] = inner
        return tuple(new)

    sums = lax.fori_loop(0, TR, conv, tuple(jnp.zeros((8, C), f32) for _ in range(9)))
    taps_part = [jnp.sum(x, axis=0, keepdims=True) for x in sums]

    @pl.loop(0, n_tm)
    def _(i):
        at = pl.ds(pl.multiple_of(i * quarter, quarter), quarter)
        value = jnp.dot(spread[at, :], point[...], preferred_element_type=f32)
        mix_send[i] = (pooled[at, :].astype(f32) + value).astype(low)
        mixed_low[at, :] = mg_recv[i]

    for step in range(1, n_tm):
        exchange(mix_send, mix_recv, mix_sems, step).start()
    mix_recv[tm] = mix_send[tm]

    def pack(first, value):
        for side in range(2):
            packed[side, first : first + value.shape[0], :] = value[
                :, side * 128 : side * 128 + 128
            ].astype(low)

    across_rows = (((0,), (0,)), ((), ()))
    pack(4 * C, lax.dot_general(spread[...], mixed_low[...], across_rows, preferred_element_type=f32))

    for copy in backward:
        copy.wait()
    edge[...] = back_recv[...].astype(f32)
    for r in range(TR):
        grad[r * TC : r * TC + 1, :] += edge[0, r : r + 1]
        grad[r * TC + TC - 1 : r * TC + TC, :] += edge[1, r : r + 1]

    def through(r, total):
        at = pl.ds(pl.multiple_of(r * TC, TC), TC)
        value = preact[at, :]
        sigma = 1.0 / (1.0 + jnp.exp(-value))
        low_grad = (grad[at, :] * (sigma * (1.0 + value * (1.0 - sigma)))).astype(low)
        pre[at, :] = low_grad
        wider = low_grad.astype(f32)
        return total + ((wider[0:8] + wider[8:16]) + (wider[16:24] + wider[24:32]))

    bias_part = lax.fori_loop(0, TR, through, jnp.zeros((8, C), f32))
    for child in range(4):
        lanes = slice(child * C, child * C + C)
        pack(child * C, jnp.dot(rows_t[lanes, :], pre[...], preferred_element_type=f32))

    for step in range(1, n_tm):
        exchange(mix_send, mix_recv, mix_sems, step).wait()

    def mixing(i, sums):
        at = pl.ds(pl.multiple_of(i * 16, 16), 16)
        cots = [cot[f, at, :].astype(f32) for f in range(n_tm)]
        mixes = [mix_recv[g, at, :].astype(f32) for g in range(n_tm)]
        new = []
        for f in range(n_tm):
            for g in range(n_tm):
                product = cots[f] * mixes[g]
                new.append(sums[n_tm * f + g] + (product[0:8] + product[8:16]))
        return tuple(new)

    sums = lax.fori_loop(
        0, quarter // 16, mixing, tuple(jnp.zeros((8, C), f32) for _ in range(n_tm * n_tm))
    )
    small = taps_part + [jnp.sum(x, axis=0, keepdims=True) for x in sums]
    small.append(jnp.sum(bias_part, axis=0, keepdims=True))
    small.append(jnp.zeros((6, C), f32))
    pack(5 * C, jnp.concatenate(small, axis=0))
    for side in range(2):
        packed[side, 1312:, :] = jnp.zeros((group * rows - 1312, 128), low)

    span = n_line * rows

    def plane_peer(step):
        index = lax.rem(mine + step, n_plane)
        return index, (index // 2 * 2 + core, line * 2 + lax.rem(index, 2))

    def line_peer(step):
        index = lax.rem(line + step, n_line)
        return index, (tm, index * 2 + lax.rem(pix, 2))

    def span_of(step):
        index, _ = plane_peer(step)
        return pl.ds(pl.multiple_of(index * span, 16), span)

    def swap(step):
        return pltpu.make_async_remote_copy(
            packed.at[1 - core, span_of(step)], core_in.at[span_of(step)],
            core_sems.at[0, step], core_sems.at[1, step], partner, MESH
        )

    def to_plane(step):
        return pltpu.make_async_remote_copy(
            half.at[span_of(step)], plane_in.at[step],
            plane_sems.at[0, step], plane_sems.at[1, step], plane_peer(step)[1], MESH
        )

    def to_line(step):
        index, device = line_peer(step)
        return pltpu.make_async_remote_copy(
            line_out.at[index], line_in.at[step],
            line_sems.at[0, step], line_sems.at[1, step], device, MESH
        )

    order = list(range(1, n_plane)) + [0]
    for step in order:
        swap(step).start()
    for step in order:
        swap(step).wait()
        at = span_of(step)
        half[at, :] = (packed[core, at, :].astype(f32) + core_in[at, :].astype(f32)).astype(low)
        if step:
            to_plane(step).start()

    for child in range(4):
        lanes = slice(child * C, child * C + C)
        value = lax.dot_general(
            pre[...], weight[lanes, :], (((1,), (1,)), ((), ())), preferred_element_type=f32
        )
        for side in range(2):
            fine[side, pl.ds(child, TR * TC, stride=4), :] = value[:, side * 128 : side * 128 + 128]

    for step in range(1, n_plane):
        to_plane(step).wait()

    def line_sum(step):
        index, _ = line_peer(step)
        at = pl.ds(pl.multiple_of(mine * span + index * rows, 16), rows)
        total = half[at, :].astype(f32)
        for other in range(1, n_plane):
            total = total + plane_in[
                other, pl.ds(pl.multiple_of(index * rows, 16), rows), :
            ].astype(f32)
        line_out[index] = total.astype(low)

    @pl.loop(1, n_line)
    def _(step):
        line_sum(step)
        to_line(step).start()

    line_sum(0)

    @pl.loop(0, 2560 // 160)
    def _(i):
        at = pl.ds(pl.multiple_of(i * 160, 160), 160)
        for side in range(2):
            result[at, side * 128 : side * 128 + 128] = fine[side, at, :].astype(low)

    store = pltpu.make_async_copy(result, out_input, out_sems.at[0])
    store.start()

    @pl.loop(1, n_line)
    def _(step):
        to_line(step).wait()

    def add(step, total):
        return total + line_in[step].astype(f32)

    def place(plane_step, line_step):
        index = lax.rem(mine + n_plane - plane_step, n_plane) * n_line + lax.rem(
            line + n_line - line_step, n_line
        )
        return full.at[core, pl.ds(pl.multiple_of(index * rows, 16), rows)]

    first = pl.ds(pl.multiple_of((mine * n_line + line) * rows, 16), rows)
    full[core, first, :] = lax.fori_loop(1, n_line, add, line_out[line].astype(f32)).astype(low)

    def back_line(step):
        return pltpu.make_async_remote_copy(
            place(0, 0), place(0, 0),
            line_back.at[0, step], line_back.at[1, step], line_peer(step)[1], MESH
        )

    def back_plane(plane_step, step):
        return pltpu.make_async_remote_copy(
            place(0, step), place(0, step), plane_send.at[plane_step, step],
            plane_recv.at[plane_step, step], plane_peer(plane_step)[1], MESH
        )

    def back_pair(plane_step, step):
        return pltpu.make_async_remote_copy(
            place(plane_step, step), place(plane_step, step), pair_send.at[plane_step, step],
            pair_recv.at[plane_step, step], partner, MESH
        )

    @pl.loop(1, n_line)
    def _(step):
        back_line(step).start()

    for plane_step in range(1, n_plane):
        back_plane(plane_step, 0).start()
    back_pair(0, 0).start()

    @pl.loop(1, n_line)
    def _(step):
        back_line(step).wait()
        for plane_step in range(1, n_plane):
            back_plane(plane_step, step).start()
        back_pair(0, step).start()

    @pl.loop(0, n_line)
    def _(step):
        for plane_step in range(1, n_plane):
            back_plane(plane_step, step).wait()
            back_pair(plane_step, step).start()

    @pl.loop(0, n_line)
    def _(step):
        for plane_step in range(n_plane):
            back_pair(plane_step, step).wait()

    store_full = pltpu.make_async_copy(full, out_full, out_sems.at[1])
    store_full.start()
    store.wait()
    store_full.wait()


def unpack_kernel(
    scale, fine_in, full_in, out_input, out_down, out_bias, out_taps, out_point, out_mix,
    full, down, bias, taps, point, mix, sems,
):
    f32 = jnp.float32
    through = pltpu.make_async_copy(fine_in, out_input, sems.at[0])
    through.start()
    load = pltpu.make_async_copy(full_in, full, sems.at[1])
    load.start()
    load.wait()
    for side in range(2):
        lanes = slice(side * 128, side * 128 + 128)
        tail = full[side, 5 * C : 5 * C + 32, :].astype(f32) * scale
        taps[:, lanes] = tail[0:9]
        for frame in range(mix.shape[0]):
            first = 9 + frame * mix.shape[1]
            mix[frame, :, lanes] = tail[first : first + mix.shape[1]]
        bias[lanes] = tail[25]
        point[:, lanes] = full[side, 4 * C : 5 * C, :].astype(f32) * scale
        down[:, lanes] = full[side, 0 : 4 * C, :].astype(f32) * scale
    stores = [
        pltpu.make_async_copy(here, there, sems.at[2 + i])
        for i, (here, there) in enumerate(
            [(down, out_down), (bias, out_bias), (taps, out_taps), (point, out_point), (mix, out_mix)]
        )
    ]
    for store in stores:
        store.start()
    for store in stores:
        store.wait()
    through.wait()


def on_device(
    activations, down_weight, down_bias, taps, point_weight, time_mix, edge_rows, cotangent
):
    frames = lax.axis_size("tm")
    tiles = lax.axis_size("pix")
    pixels = TR * TC
    quarter = pixels // frames
    scale = 1.0 / math.sqrt(frames * tiles * pixels)
    group = frames // 2 * tiles
    rows = -(-1312 // (16 * group)) * 16
    f32, low = jnp.float32, jnp.bfloat16
    both = lambda n: pltpu.SemaphoreType.DMA((2, n))
    n_plane, n_line = frames // 2 * 2, tiles // 2
    grid = pltpu.SemaphoreType.DMA((n_plane, n_line))
    hbm = pl.BlockSpec(memory_space=pltpu.HBM)
    fine, full = pl.pallas_call(
        functools.partial(kernel, rows),
        out_shape=[
            jax.ShapeDtypeStruct((4 * pixels, C), low),
            jax.ShapeDtypeStruct((2, group * rows, 128), low),
        ],
        in_specs=[hbm] * 8,
        out_specs=[hbm] * 2,
        scratch_shapes=[
            pltpu.VMEM((4 * pixels, C), low),
            pltpu.VMEM((4 * C, C), low),
            pltpu.VMEM((1, C), f32),
            pltpu.VMEM((9, C), f32),
            pltpu.VMEM((C, C), low),
            pltpu.VMEM((frames, frames, C), f32),
            pltpu.VMEM((1, 2, TR), jnp.int32),
            pltpu.VMEM((frames, quarter, C), low),
            pltpu.VMEM((2, 32, 32), f32),
            pltpu.VMEM((4 * pixels, C), low),
            pltpu.VMEM((2, 4 * pixels, 128), f32),
            pltpu.VMEM((pixels, 4 * C), low),
            pltpu.VMEM((4 * C, pixels), low),
            pltpu.VMEM((pixels, C), f32),
            pltpu.VMEM((pixels, C), low),
            pltpu.VMEM((3, TR + 2, TC, C), f32),
            pltpu.VMEM((3, TR + 2, TC, C), f32),
            pltpu.VMEM((pixels, C), f32),
            pltpu.VMEM((pixels, C), low),
            pltpu.VMEM((pixels, C), low),
            pltpu.VMEM((frames, quarter, C), low),
            pltpu.VMEM((frames, quarter, C), low),
            pltpu.VMEM((frames, quarter, C), low),
            pltpu.VMEM((frames, quarter, C), low),
            pltpu.VMEM((2, 32, C), f32),
            pltpu.VMEM((2, 32, C), low),
            pltpu.VMEM((2, 32, C), low),
            pltpu.VMEM((2, 32, C), low),
            pltpu.VMEM((2, 32, C), low),
            pltpu.VMEM((pixels, C), low),
            pltpu.VMEM((2, group * rows, 128), low),
            pltpu.VMEM((group * rows, 128), low),
            pltpu.VMEM((group * rows, 128), low),
            pltpu.VMEM((n_plane, n_line * rows, 128), low),
            pltpu.VMEM((n_line, rows, 128), low),
            pltpu.VMEM((n_line, rows, 128), low),
            pltpu.VMEM((2, group * rows, 128), low),
            pltpu.SemaphoreType.DMA((8,)),
            pltpu.SemaphoreType.DMA((2,)),
            both(frames), both(frames), both(2), both(2),
            both(n_plane), both(n_plane), both(n_line), both(n_line), grid, grid, grid, grid,
        ],
        compiler_params=pltpu.CompilerParams(
            collective_id=0, has_side_effects=True, vmem_limit_bytes=48 * 1024 * 1024
        ),
    )(
        activations.reshape(4 * pixels, C),
        down_weight,
        down_bias.reshape(1, C),
        taps,
        point_weight,
        time_mix,
        edge_rows,
        cotangent,
    )
    shapes = [(4 * C, C), (C,), (9, C), (C, C), (frames, frames, C)]
    outs = pl.pallas_call(
        functools.partial(unpack_kernel, scale),
        out_shape=[jax.ShapeDtypeStruct((4 * pixels, C), low)]
        + [jax.ShapeDtypeStruct(shape, f32) for shape in shapes],
        in_specs=[hbm] * 2,
        out_specs=[hbm] * 6,
        scratch_shapes=[pltpu.VMEM((2, group * rows, 128), low)]
        + [pltpu.VMEM(shape, f32) for shape in shapes]
        + [pltpu.SemaphoreType.DMA((7,))],
        compiler_params=pltpu.CompilerParams(vmem_limit_bytes=32 * 1024 * 1024),
    )(fine, full)
    return (outs[0].reshape(1, 4 * pixels, C), *outs[1:])


def solution(mesh):
    in_specs = (
        P("tm", "pix", None),
        P(),
        P(),
        P(),
        P(),
        P(),
        P("pix", None, None),
        P(None, ("pix", "tm"), None),
    )
    out_specs = (P("tm", "pix", None), P(), P(), P(), P(), P())
    return jax.shard_map(
        on_device, mesh=mesh, in_specs=in_specs, out_specs=out_specs, check_vma=False
    )
```

```python
import functools
import math

import jax
import jax.numpy as jnp
from jax import lax
from jax.experimental import pallas as pl
from jax.experimental.pallas import tpu as pltpu
from jax.sharding import PartitionSpec as P

C = 256
TR = 20
TC = 32
MESH = pl.DeviceIdType.MESH


def kernel(
    rows, rest_rows, act_in, weight_in, bias_in, taps_in, point_in, mix_in, maps_in, cot_in,
    out_input, out_full,
    act, weight, bias, taps, point, mix, maps, cot, perm, result,
    fine, rows_in, rows_t, preact, pooled, wide, gwide, grad, spread, mixed_low,
    mg_send, mg_recv, mix_send, mix_recv, edge, edge_send, edge_recv, back_send, back_recv, pre,
    packed, core_in, half, full, plane_in, line_out, line_in, rest_plane_in, rest_line_out, rest_line_in,
    in_sems, out_sems, mg_sems, mix_sems, edge_sems, back_sems,
    *total_sems,
):
    f32, low = jnp.float32, jnp.bfloat16
    tm, pix = lax.axis_index("tm"), lax.axis_index("pix")
    n_tm, n_pix = lax.axis_size("tm"), lax.axis_size("pix")
    group = n_tm // 2 * n_pix
    core = lax.rem(tm, 2)
    me = tm // 2 * n_pix + pix
    n_plane, n_line = n_tm // 2 * 2, n_pix // 2
    mine, line = tm // 2 * 2 + lax.rem(pix, 2), pix // 2
    partner = (tm + 1 - 2 * core, pix)
    west, east = (tm, lax.rem(pix + n_pix - 1, n_pix)), (tm, lax.rem(pix + 1, n_pix))
    quarter = TR * TC // n_tm

    def peer(step):
        index = lax.rem(me + step, group)
        return index, (index // n_pix * 2 + core, lax.rem(index, n_pix))

    loads = [
        pltpu.make_async_copy(there, here, in_sems.at[i])
        for i, (there, here) in enumerate(
            [
                (cot_in, cot), (mix_in, mix), (act_in, act), (weight_in, weight), (bias_in, bias),
                (point_in, point), (taps_in, taps), (maps_in, maps),
            ]
        )
    ]
    for load in loads:
        load.start()

    barrier = pltpu.get_barrier_semaphore()
    pl.semaphore_signal(barrier, inc=1, device_id=partner, device_id_type=MESH)
    across = (lax.rem(partner[0] + 2, n_tm), pix)
    pl.semaphore_signal(barrier, inc=1, device_id=across, device_id_type=MESH)

    @pl.loop(1, group)
    def _(step):
        _, device = peer(step)
        pl.semaphore_signal(barrier, inc=1, device_id=device, device_id_type=MESH)

    loads[0].wait()
    loads[1].wait()
    for frame in range(n_tm):
        total = mix[0, frame : frame + 1] * cot[0].astype(f32)
        for source in range(1, n_tm):
            total = total + mix[source, frame : frame + 1] * cot[source].astype(f32)
        mg_send[frame] = total.astype(low)
    pl.semaphore_wait(barrier, group + 1)

    def exchange(send, recv, sems, step):
        target = lax.rem(tm + step, n_tm)
        return pltpu.make_async_remote_copy(
            send.at[target], recv.at[tm], sems.at[0, step], sems.at[1, step], (target, pix), MESH
        )

    for step in range(1, n_tm):
        exchange(mg_send, mg_recv, mg_sems, step).start()
    mg_recv[tm] = mg_send[tm]

    for load in loads[2:]:
        load.wait()
    perm[...] = jnp.zeros(perm.shape, f32)
    for side in range(2):
        row = lax.broadcasted_iota(jnp.int32, (TR, TR), 0)
        perm[side, 0:TR, 0:TR] = jnp.where(maps[0, side : side + 1, :] == row, 1.0, 0.0)

    @pl.loop(0, 2560 // 160)
    def _(i):
        at = pl.ds(pl.multiple_of(i * 160, 160), 160)
        for side in range(2):
            fine[side, at, :] = act[at, side * 128 : side * 128 + 128].astype(f32)

    for child in range(4):
        for side in range(2):
            lanes = slice(child * C + side * 128, child * C + side * 128 + 128)
            rows_in[:, lanes] = fine[side, pl.ds(child, TR * TC, stride=4), :].astype(low)

    @pl.loop(0, 4)
    def _(i):
        at = pl.ds(pl.multiple_of(i * 160, 160), 160)
        value = jnp.dot(rows_in[at, :], weight[...], preferred_element_type=f32) + bias[...]
        preact[at, :] = value
        pooled[at, :] = (value / (1.0 + jnp.exp(-value))).astype(low)

    def shifted(ref, values, r):
        ref[1, r + 1] = values
        ref[0, r + 1, 1:TC, :] = values[0 : TC - 1]
        ref[2, r + 1, 0 : TC - 1, :] = values[1:TC]

    for side in range(3):
        for r in (0, TR + 1):
            wide[side, r] = jnp.zeros((TC, C), f32)
            gwide[side, r] = jnp.zeros((TC, C), f32)

    @pl.loop(0, TR)
    def _(r):
        shifted(wide, pooled[pl.ds(pl.multiple_of(r * TC, TC), TC), :].astype(f32), r)

    edge[...] = jnp.zeros(edge.shape, f32)
    for r in range(TR):
        edge[0, r : r + 1] = wide[1, r + 1, 0:1, :]
        edge[1, r : r + 1] = wide[1, r + 1, TC - 1 : TC, :]
    edge_send[...] = edge[...].astype(low)

    def swap_edges(send, recv, sems):
        return [
            pltpu.make_async_remote_copy(
                send.at[0], recv.at[1], sems.at[0, 0], sems.at[1, 0], west, MESH
            ),
            pltpu.make_async_remote_copy(
                send.at[1], recv.at[0], sems.at[0, 1], sems.at[1, 1], east, MESH
            ),
        ]

    forward = swap_edges(edge_send, edge_recv, edge_sems)
    for copy in forward:
        copy.start()

    for child in range(4):
        lanes = slice(child * C, child * C + C)
        rows_t[lanes, :] = rows_in[:, lanes].T

    for step in range(1, n_tm):
        exchange(mg_send, mg_recv, mg_sems, step).wait()

    @pl.loop(0, n_tm)
    def _(i):
        value = lax.dot_general(
            mg_recv[i], point[...], (((1,), (1,)), ((), ())), preferred_element_type=f32
        )
        pre[pl.ds(pl.multiple_of(i * quarter, quarter), quarter), :] = value.astype(low)

    @pl.loop(0, TR)
    def _(r):
        shifted(gwide, pre[pl.ds(pl.multiple_of(r * TC, TC), TC), :].astype(f32), r)
        gwide[0, r + 1, 0:1, :] = jnp.zeros((1, C), f32)
        gwide[2, r + 1, TC - 1 : TC, :] = jnp.zeros((1, C), f32)

    edge[...] = jnp.zeros(edge.shape, f32)
    for r in range(TR):
        edge[0, r + 1 : r + 2] = gwide[1, r + 1, 0:1, :]
        edge[1, r + 1 : r + 2] = gwide[1, r + 1, TC - 1 : TC, :]
    for side in range(2):
        total = jnp.zeros((TR, C), f32)
        for a in range(3):
            tap = 3 * a + 2 * side
            total = total + taps[tap : tap + 1] * edge[side, 2 - a : 2 - a + TR]
        total = jnp.concatenate([total, jnp.zeros((32 - TR, C), f32)], axis=0).astype(low)
        back_send[side] = jnp.dot(perm[side].astype(low), total, preferred_element_type=f32).astype(low)
    backward = swap_edges(back_send, back_recv, back_sems)
    for copy in backward:
        copy.start()

    def pack(first, value):
        for side in range(2):
            packed[side, first : first + value.shape[0], :] = value[
                :, side * 128 : side * 128 + 128
            ].astype(low)

    def inner(r, carry):
        value = mg_recv[r // (TR // n_tm), pl.ds(
            pl.multiple_of(lax.rem(r, TR // n_tm) * TC, TC), TC
        ), :].astype(f32)
        for a in range(3):
            for b in range(3):
                value = value + taps[3 * a + b : 3 * a + b + 1] * gwide[2 - b, r + 2 - a]
        grad[pl.ds(pl.multiple_of(r * TC, TC), TC), :] = value
        return carry

    lax.fori_loop(0, TR, inner, 0)
    for copy in backward:
        copy.wait()
    edge[...] = back_recv[...].astype(f32)
    for r in range(TR):
        grad[r * TC : r * TC + 1, :] += edge[0, r : r + 1]
        grad[r * TC + TC - 1 : r * TC + TC, :] += edge[1, r : r + 1]

    def through(r, total):
        at = pl.ds(pl.multiple_of(r * TC, TC), TC)
        value = preact[at, :]
        sigma = 1.0 / (1.0 + jnp.exp(-value))
        low_grad = (grad[at, :] * (sigma * (1.0 + value * (1.0 - sigma)))).astype(low)
        pre[at, :] = low_grad
        wider = low_grad.astype(f32)
        return total + ((wider[0:8] + wider[8:16]) + (wider[16:24] + wider[24:32]))

    bias_part = lax.fori_loop(0, TR, through, jnp.zeros((8, C), f32))
    for child in range(4):
        lanes = slice(child * C, child * C + C)
        pack(child * C, jnp.dot(rows_t[lanes, :], pre[...], preferred_element_type=f32))
    size = group * rows
    for side in range(2):
        if size > 4 * C:
            packed[side, 4 * C : size, :] = jnp.zeros((size - 4 * C, 128), low)

    def plane_peer(step):
        index = lax.rem(mine + step, n_plane)
        return index, (index // 2 * 2 + core, line * 2 + lax.rem(index, 2))

    def line_peer(step):
        index = lax.rem(line + step, n_line)
        return index, (tm, index * 2 + lax.rem(pix, 2))

    def total_stages(base, rows, plane_in, line_out, line_in, sems):
        core_sems, plane_sems, line_sems, line_back, plane_send, plane_recv, pair_send, pair_recv = sems
        span = n_line * rows
        order = list(range(1, n_plane)) + [0]

        def span_of(step):
            return pl.ds(pl.multiple_of(base + plane_peer(step)[0] * span, 16), span)

        def swap(step):
            return pltpu.make_async_remote_copy(
                packed.at[1 - core, span_of(step)], core_in.at[span_of(step)],
                core_sems.at[0, step], core_sems.at[1, step], partner, MESH
            )

        def to_plane(step):
            return pltpu.make_async_remote_copy(
                half.at[span_of(step)], plane_in.at[step],
                plane_sems.at[0, step], plane_sems.at[1, step], plane_peer(step)[1], MESH
            )

        def to_line(step):
            index, device = line_peer(step)
            return pltpu.make_async_remote_copy(
                line_out.at[index], line_in.at[step],
                line_sems.at[0, step], line_sems.at[1, step], device, MESH
            )

        def place(plane_step, line_step):
            index = lax.rem(mine + n_plane - plane_step, n_plane) * n_line + lax.rem(
                line + n_line - line_step, n_line
            )
            return full.at[core, pl.ds(pl.multiple_of(base + index * rows, 16), rows)]

        def back_line(step):
            return pltpu.make_async_remote_copy(
                place(0, 0), place(0, 0),
                line_back.at[0, step], line_back.at[1, step], line_peer(step)[1], MESH
            )

        def back_plane(plane_step, step):
            return pltpu.make_async_remote_copy(
                place(0, step), place(0, step), plane_send.at[plane_step, step],
                plane_recv.at[plane_step, step], plane_peer(plane_step)[1], MESH
            )

        def back_pair(plane_step, step):
            return pltpu.make_async_remote_copy(
                place(plane_step, step), place(plane_step, step), pair_send.at[plane_step, step],
                pair_recv.at[plane_step, step], partner, MESH
            )

        def start():
            for step in order:
                swap(step).start()

        def enter_plane():
            for step in order:
                swap(step).wait()
                at = span_of(step)
                half[at, :] = (packed[core, at, :].astype(f32) + core_in[at, :].astype(f32)).astype(
                    low
                )
                if step:
                    to_plane(step).start()

        def enter_line():
            for step in range(1, n_plane):
                to_plane(step).wait()

            def line_sum(step):
                index, _ = line_peer(step)
                at = pl.ds(pl.multiple_of(base + mine * span + index * rows, 16), rows)
                total = half[at, :].astype(f32)
                for other in range(1, n_plane):
                    total = total + plane_in[
                        other, pl.ds(pl.multiple_of(index * rows, 16), rows), :
                    ].astype(f32)
                line_out[index] = total.astype(low)

            @pl.loop(1, n_line)
            def _(step):
                line_sum(step)
                to_line(step).start()

            line_sum(0)

        def turn():
            @pl.loop(1, n_line)
            def _(step):
                to_line(step).wait()

            def add(step, total):
                return total + line_in[step].astype(f32)

            first = pl.ds(pl.multiple_of(base + (mine * n_line + line) * rows, 16), rows)
            full[core, first, :] = lax.fori_loop(
                1, n_line, add, line_out[line].astype(f32)
            ).astype(low)

            @pl.loop(1, n_line)
            def _(step):
                back_line(step).start()

            for plane_step in range(1, n_plane):
                back_plane(plane_step, 0).start()
            back_pair(0, 0).start()

        def leave_line():
            @pl.loop(1, n_line)
            def _(step):
                back_line(step).wait()
                for plane_step in range(1, n_plane):
                    back_plane(plane_step, step).start()
                back_pair(0, step).start()

        def leave_plane():
            @pl.loop(0, n_line)
            def _(step):
                for plane_step in range(1, n_plane):
                    back_plane(plane_step, step).wait()
                    back_pair(plane_step, step).start()

        def finish():
            @pl.loop(0, n_line)
            def _(step):
                for plane_step in range(n_plane):
                    back_pair(plane_step, step).wait()

        return start, enter_plane, enter_line, turn, leave_line, leave_plane, finish

    down = total_stages(0, rows, plane_in, line_out, line_in, total_sems[:8])
    rest = total_stages(
        size, rest_rows, rest_plane_in, rest_line_out, rest_line_in, total_sems[8:]
    )
    down[0]()

    for copy in forward:
        copy.wait()
    for side in range(2):
        edge[side] = jnp.dot(
            perm[side].astype(low), edge_recv[side], preferred_element_type=f32
        )
    for r in range(TR):
        wide[0, r + 1, 0:1, :] = edge[0, r : r + 1]
        wide[2, r + 1, TC - 1 : TC, :] = edge[1, r : r + 1]
    down[1]()

    def conv(r, sums):
        total = jnp.zeros((TC, C), f32)
        here = gwide[1, r + 1]
        new = []
        for a in range(3):
            for b in range(3):
                cells = wide[b, r + a]
                total = total + taps[3 * a + b : 3 * a + b + 1] * cells
                product = here * cells
                new.append(
                    sums[3 * a + b]
                    + ((product[0:8] + product[8:16]) + (product[16:24] + product[24:32]))
                )
        spread[pl.ds(pl.multiple_of(r * TC, TC), TC), :] = total.astype(low)
        return tuple(new)

    sums = lax.fori_loop(0, TR, conv, tuple(jnp.zeros((8, C), f32) for _ in range(9)))
    small = [jnp.sum(x, axis=0, keepdims=True) for x in sums]

    @pl.loop(0, n_tm)
    def _(i):
        at = pl.ds(pl.multiple_of(i * quarter, quarter), quarter)
        value = jnp.dot(spread[at, :], point[...], preferred_element_type=f32)
        mix_send[i] = (pooled[at, :].astype(f32) + value).astype(low)
        mixed_low[at, :] = mg_recv[i]

    for step in range(1, n_tm):
        exchange(mix_send, mix_recv, mix_sems, step).start()
    mix_recv[tm] = mix_send[tm]
    down[2]()

    across_rows = (((0,), (0,)), ((), ()))
    pack(size, lax.dot_general(spread[...], mixed_low[...], across_rows, preferred_element_type=f32))
    down[3]()

    for step in range(1, n_tm):
        exchange(mix_send, mix_recv, mix_sems, step).wait()

    def mixing(i, sums):
        at = pl.ds(pl.multiple_of(i * 16, 16), 16)
        cots = [cot[f, at, :].astype(f32) for f in range(n_tm)]
        mixes = [mix_recv[g, at, :].astype(f32) for g in range(n_tm)]
        new = []
        for f in range(n_tm):
            for g in range(n_tm):
                product = cots[f] * mixes[g]
                new.append(sums[n_tm * f + g] + (product[0:8] + product[8:16]))
        return tuple(new)

    sums = lax.fori_loop(
        0, quarter // 16, mixing, tuple(jnp.zeros((8, C), f32) for _ in range(n_tm * n_tm))
    )
    small += [jnp.sum(x, axis=0, keepdims=True) for x in sums]
    small.append(jnp.sum(bias_part, axis=0, keepdims=True))
    small.append(jnp.zeros((6, C), f32))
    pack(size + C, jnp.concatenate(small, axis=0))
    for side in range(2):
        packed[side, size + C + 32 :, :] = jnp.zeros((group * rest_rows - C - 32, 128), low)
    rest[0]()
    down[4]()

    for child in range(4):
        lanes = slice(child * C, child * C + C)
        value = lax.dot_general(
            pre[...], weight[lanes, :], (((1,), (1,)), ((), ())), preferred_element_type=f32
        )
        for side in range(2):
            fine[side, pl.ds(child, TR * TC, stride=4), :] = value[:, side * 128 : side * 128 + 128]
    rest[1]()

    @pl.loop(0, 2560 // 160)
    def _(i):
        at = pl.ds(pl.multiple_of(i * 160, 160), 160)
        for side in range(2):
            result[at, side * 128 : side * 128 + 128] = fine[side, at, :].astype(low)

    store = pltpu.make_async_copy(result, out_input, out_sems.at[0])
    store.start()
    rest[2]()
    down[5]()
    rest[3]()
    down[6]()
    store_down = pltpu.make_async_copy(
        full.at[:, 0:size], out_full.at[:, 0:size], out_sems.at[1]
    )
    store_down.start()
    for stage in rest[4:]:
        stage()
    store_rest = pltpu.make_async_copy(
        full.at[:, size:], out_full.at[:, size:], out_sems.at[2]
    )
    store_rest.start()
    store.wait()
    store_down.wait()
    store_rest.wait()


def unpack_kernel(
    scale, size, fine_in, full_in, out_input, out_down, out_bias, out_taps, out_point, out_mix,
    full, down, bias, taps, point, mix, sems,
):
    f32 = jnp.float32
    through = pltpu.make_async_copy(fine_in, out_input, sems.at[0])
    through.start()
    load = pltpu.make_async_copy(full_in, full, sems.at[1])
    load.start()
    load.wait()
    for side in range(2):
        lanes = slice(side * 128, side * 128 + 128)
        tail = full[side, size + C : size + C + 32, :].astype(f32) * scale
        taps[:, lanes] = tail[0:9]
        for frame in range(mix.shape[0]):
            first = 9 + frame * mix.shape[1]
            mix[frame, :, lanes] = tail[first : first + mix.shape[1]]
        bias[lanes] = tail[25]
        point[:, lanes] = full[side, size : size + C, :].astype(f32) * scale
        down[:, lanes] = full[side, 0 : 4 * C, :].astype(f32) * scale
    stores = [
        pltpu.make_async_copy(here, there, sems.at[2 + i])
        for i, (here, there) in enumerate(
            [(down, out_down), (bias, out_bias), (taps, out_taps), (point, out_point), (mix, out_mix)]
        )
    ]
    for store in stores:
        store.start()
    for store in stores:
        store.wait()
    through.wait()


def on_device(
    activations, down_weight, down_bias, taps, point_weight, time_mix, edge_rows, cotangent
):
    frames = lax.axis_size("tm")
    tiles = lax.axis_size("pix")
    pixels = TR * TC
    quarter = pixels // frames
    scale = 1.0 / math.sqrt(frames * tiles * pixels)
    group = frames // 2 * tiles
    rows = -(-4 * C // (16 * group)) * 16
    rest_rows = -(-(C + 32) // (16 * group)) * 16
    size = group * (rows + rest_rows)
    f32, low = jnp.float32, jnp.bfloat16
    both = lambda n: pltpu.SemaphoreType.DMA((2, n))
    n_plane, n_line = frames // 2 * 2, tiles // 2
    grid = pltpu.SemaphoreType.DMA((n_plane, n_line))
    hbm = pl.BlockSpec(memory_space=pltpu.HBM)
    fine, full = pl.pallas_call(
        functools.partial(kernel, rows, rest_rows),
        out_shape=[
            jax.ShapeDtypeStruct((4 * pixels, C), low),
            jax.ShapeDtypeStruct((2, size, 128), low),
        ],
        in_specs=[hbm] * 8,
        out_specs=[hbm] * 2,
        scratch_shapes=[
            pltpu.VMEM((4 * pixels, C), low),
            pltpu.VMEM((4 * C, C), low),
            pltpu.VMEM((1, C), f32),
            pltpu.VMEM((9, C), f32),
            pltpu.VMEM((C, C), low),
            pltpu.VMEM((frames, frames, C), f32),
            pltpu.VMEM((1, 2, TR), jnp.int32),
            pltpu.VMEM((frames, quarter, C), low),
            pltpu.VMEM((2, 32, 32), f32),
            pltpu.VMEM((4 * pixels, C), low),
            pltpu.VMEM((2, 4 * pixels, 128), f32),
            pltpu.VMEM((pixels, 4 * C), low),
            pltpu.VMEM((4 * C, pixels), low),
            pltpu.VMEM((pixels, C), f32),
            pltpu.VMEM((pixels, C), low),
            pltpu.VMEM((3, TR + 2, TC, C), f32),
            pltpu.VMEM((3, TR + 2, TC, C), f32),
            pltpu.VMEM((pixels, C), f32),
            pltpu.VMEM((pixels, C), low),
            pltpu.VMEM((pixels, C), low),
            pltpu.VMEM((frames, quarter, C), low),
            pltpu.VMEM((frames, quarter, C), low),
            pltpu.VMEM((frames, quarter, C), low),
            pltpu.VMEM((frames, quarter, C), low),
            pltpu.VMEM((2, 32, C), f32),
            pltpu.VMEM((2, 32, C), low),
            pltpu.VMEM((2, 32, C), low),
            pltpu.VMEM((2, 32, C), low),
            pltpu.VMEM((2, 32, C), low),
            pltpu.VMEM((pixels, C), low),
            pltpu.VMEM((2, size, 128), low),
            pltpu.VMEM((size, 128), low),
            pltpu.VMEM((size, 128), low),
            pltpu.VMEM((2, size, 128), low),
            pltpu.VMEM((n_plane, n_line * rows, 128), low),
            pltpu.VMEM((n_line, rows, 128), low),
            pltpu.VMEM((n_line, rows, 128), low),
            pltpu.VMEM((n_plane, n_line * rest_rows, 128), low),
            pltpu.VMEM((n_line, rest_rows, 128), low),
            pltpu.VMEM((n_line, rest_rows, 128), low),
            pltpu.SemaphoreType.DMA((8,)),
            pltpu.SemaphoreType.DMA((3,)),
            both(frames), both(frames), both(2), both(2),
        ]
        + 2 * [both(n_plane), both(n_plane), both(n_line), both(n_line), grid, grid, grid, grid],
        compiler_params=pltpu.CompilerParams(
            collective_id=0, has_side_effects=True, vmem_limit_bytes=64 * 1024 * 1024
        ),
    )(
        activations.reshape(4 * pixels, C),
        down_weight,
        down_bias.reshape(1, C),
        taps,
        point_weight,
        time_mix,
        edge_rows,
        cotangent,
    )
    shapes = [(4 * C, C), (C,), (9, C), (C, C), (frames, frames, C)]
    outs = pl.pallas_call(
        functools.partial(unpack_kernel, scale, group * rows),
        out_shape=[jax.ShapeDtypeStruct((4 * pixels, C), low)]
        + [jax.ShapeDtypeStruct(shape, f32) for shape in shapes],
        in_specs=[hbm] * 2,
        out_specs=[hbm] * 6,
        scratch_shapes=[pltpu.VMEM((2, size, 128), low)]
        + [pltpu.VMEM(shape, f32) for shape in shapes]
        + [pltpu.SemaphoreType.DMA((7,))],
        compiler_params=pltpu.CompilerParams(vmem_limit_bytes=64 * 1024 * 1024),
    )(fine, full)
    return (outs[0].reshape(1, 4 * pixels, C), *outs[1:])


def solution(mesh):
    in_specs = (
        P("tm", "pix", None),
        P(),
        P(),
        P(),
        P(),
        P(),
        P("pix", None, None),
        P(None, ("pix", "tm"), None),
    )
    out_specs = (P("tm", "pix", None), P(), P(), P(), P(), P())
    return jax.shard_map(
        on_device, mesh=mesh, in_specs=in_specs, out_specs=out_specs, check_vma=False
    )
```

```python
import functools
import math

import jax
import jax.numpy as jnp
from jax import lax
from jax.experimental import pallas as pl
from jax.experimental.pallas import tpu as pltpu
from jax.sharding import PartitionSpec as P

C = 256
TR = 20
TC = 32
MESH = pl.DeviceIdType.MESH


def kernel(
    rows, rest_rows, act_in, weight_in, bias_in, taps_in, point_in, mix_in, maps_in, cot_in,
    out_input, out_full,
    act, weight, bias, taps, point, mix, maps, cot, perm, result,
    fine, rows_in, rows_t, preact, pooled, wide, gwide, grad, spread, mixed_low,
    mg_send, mg_recv, mix_send, mix_recv, edge, edge_send, edge_recv, back_send, back_recv, pre,
    packed, core_in, half, full, plane_in, line_out, line_in, rest_plane_in, rest_line_out, rest_line_in,
    in_sems, out_sems, mg_sems, mix_sems, edge_sems, back_sems,
    *total_sems,
):
    f32, low = jnp.float32, jnp.bfloat16
    tm, pix = lax.axis_index("tm"), lax.axis_index("pix")
    n_tm, n_pix = lax.axis_size("tm"), lax.axis_size("pix")
    group = n_tm // 2 * n_pix
    core = lax.rem(tm, 2)
    me = tm // 2 * n_pix + pix
    n_plane, n_line = n_tm // 2 * 2, n_pix // 2
    mine, line = tm // 2 * 2 + lax.rem(pix, 2), pix // 2
    partner = (tm + 1 - 2 * core, pix)
    west, east = (tm, lax.rem(pix + n_pix - 1, n_pix)), (tm, lax.rem(pix + 1, n_pix))
    quarter = TR * TC // n_tm

    def peer(step):
        index = lax.rem(me + step, group)
        return index, (index // n_pix * 2 + core, lax.rem(index, n_pix))

    loads = [
        pltpu.make_async_copy(there, here, in_sems.at[i])
        for i, (there, here) in enumerate(
            [
                (cot_in, cot), (mix_in, mix), (act_in, act), (weight_in, weight), (bias_in, bias),
                (point_in, point), (taps_in, taps), (maps_in, maps),
            ]
        )
    ]
    for load in loads:
        load.start()

    barrier = pltpu.get_barrier_semaphore()
    pl.semaphore_signal(barrier, inc=1, device_id=partner, device_id_type=MESH)
    across = (lax.rem(partner[0] + 2, n_tm), pix)
    pl.semaphore_signal(barrier, inc=1, device_id=across, device_id_type=MESH)

    @pl.loop(1, group)
    def _(step):
        _, device = peer(step)
        pl.semaphore_signal(barrier, inc=1, device_id=device, device_id_type=MESH)

    loads[0].wait()
    loads[1].wait()
    for frame in range(n_tm):
        total = mix[0, frame : frame + 1] * cot[0].astype(f32)
        for source in range(1, n_tm):
            total = total + mix[source, frame : frame + 1] * cot[source].astype(f32)
        mg_send[frame] = total.astype(low)
    pl.semaphore_wait(barrier, group + 1)

    def exchange(send, recv, sems, step):
        target = lax.rem(tm + step, n_tm)
        return pltpu.make_async_remote_copy(
            send.at[target], recv.at[tm], sems.at[0, step], sems.at[1, step], (target, pix), MESH
        )

    for step in range(1, n_tm):
        exchange(mg_send, mg_recv, mg_sems, step).start()
    mg_recv[tm] = mg_send[tm]

    for load in loads[2:]:
        load.wait()
    perm[...] = jnp.zeros(perm.shape, f32)
    for side in range(2):
        row = lax.broadcasted_iota(jnp.int32, (TR, TR), 0)
        perm[side, 0:TR, 0:TR] = jnp.where(maps[0, side : side + 1, :] == row, 1.0, 0.0)

    @pl.loop(0, 2560 // 160)
    def _(i):
        at = pl.ds(pl.multiple_of(i * 160, 160), 160)
        for side in range(2):
            fine[side, at, :] = act[at, side * 128 : side * 128 + 128].astype(f32)

    for child in range(4):
        for side in range(2):
            lanes = slice(child * C + side * 128, child * C + side * 128 + 128)
            rows_in[:, lanes] = fine[side, pl.ds(child, TR * TC, stride=4), :].astype(low)

    @pl.loop(0, 4)
    def _(i):
        at = pl.ds(pl.multiple_of(i * 160, 160), 160)
        value = jnp.dot(rows_in[at, :], weight[...], preferred_element_type=f32) + bias[...]
        preact[at, :] = value
        pooled[at, :] = (value / (1.0 + jnp.exp(-value))).astype(low)

    def shifted(ref, values, r):
        ref[1, r + 1] = values
        ref[0, r + 1, 1:TC, :] = values[0 : TC - 1]
        ref[2, r + 1, 0 : TC - 1, :] = values[1:TC]

    for side in range(3):
        for r in (0, TR + 1):
            wide[side, r] = jnp.zeros((TC, C), f32)
            gwide[side, r] = jnp.zeros((TC, C), f32)

    @pl.loop(0, TR)
    def _(r):
        shifted(wide, pooled[pl.ds(pl.multiple_of(r * TC, TC), TC), :].astype(f32), r)

    edge[...] = jnp.zeros(edge.shape, f32)
    for r in range(TR):
        edge[0, r : r + 1] = wide[1, r + 1, 0:1, :]
        edge[1, r : r + 1] = wide[1, r + 1, TC - 1 : TC, :]
    edge_send[...] = edge[...].astype(low)

    def swap_edges(send, recv, sems):
        return [
            pltpu.make_async_remote_copy(
                send.at[0], recv.at[1], sems.at[0, 0], sems.at[1, 0], west, MESH
            ),
            pltpu.make_async_remote_copy(
                send.at[1], recv.at[0], sems.at[0, 1], sems.at[1, 1], east, MESH
            ),
        ]

    forward = swap_edges(edge_send, edge_recv, edge_sems)
    for copy in forward:
        copy.start()

    for child in range(4):
        lanes = slice(child * C, child * C + C)
        rows_t[lanes, :] = rows_in[:, lanes].T

    for step in range(1, n_tm):
        exchange(mg_send, mg_recv, mg_sems, step).wait()

    @pl.loop(0, n_tm)
    def _(i):
        value = lax.dot_general(
            mg_recv[i], point[...], (((1,), (1,)), ((), ())), preferred_element_type=f32
        )
        pre[pl.ds(pl.multiple_of(i * quarter, quarter), quarter), :] = value.astype(low)

    @pl.loop(0, TR)
    def _(r):
        shifted(gwide, pre[pl.ds(pl.multiple_of(r * TC, TC), TC), :].astype(f32), r)
        gwide[0, r + 1, 0:1, :] = jnp.zeros((1, C), f32)
        gwide[2, r + 1, TC - 1 : TC, :] = jnp.zeros((1, C), f32)

    edge[...] = jnp.zeros(edge.shape, f32)
    for r in range(TR):
        edge[0, r + 1 : r + 2] = gwide[1, r + 1, 0:1, :]
        edge[1, r + 1 : r + 2] = gwide[1, r + 1, TC - 1 : TC, :]
    for side in range(2):
        total = jnp.zeros((TR, C), f32)
        for a in range(3):
            tap = 3 * a + 2 * side
            total = total + taps[tap : tap + 1] * edge[side, 2 - a : 2 - a + TR]
        total = jnp.concatenate([total, jnp.zeros((32 - TR, C), f32)], axis=0).astype(low)
        back_send[side] = jnp.dot(perm[side].astype(low), total, preferred_element_type=f32).astype(low)
    backward = swap_edges(back_send, back_recv, back_sems)
    for copy in backward:
        copy.start()

    def pack(first, value):
        for side in range(2):
            packed[side, first : first + value.shape[0], :] = value[
                :, side * 128 : side * 128 + 128
            ].astype(low)

    def inner(r, carry):
        value = mg_recv[r // (TR // n_tm), pl.ds(
            pl.multiple_of(lax.rem(r, TR // n_tm) * TC, TC), TC
        ), :].astype(f32)
        for a in range(3):
            for b in range(3):
                value = value + taps[3 * a + b : 3 * a + b + 1] * gwide[2 - b, r + 2 - a]
        grad[pl.ds(pl.multiple_of(r * TC, TC), TC), :] = value
        return carry

    lax.fori_loop(0, TR, inner, 0, unroll=2)
    for copy in backward:
        copy.wait()
    edge[...] = back_recv[...].astype(f32)
    for r in range(TR):
        grad[r * TC : r * TC + 1, :] += edge[0, r : r + 1]
        grad[r * TC + TC - 1 : r * TC + TC, :] += edge[1, r : r + 1]

    def through(r, total):
        at = pl.ds(pl.multiple_of(r * TC, TC), TC)
        value = preact[at, :]
        sigma = 1.0 / (1.0 + jnp.exp(-value))
        low_grad = (grad[at, :] * (sigma * (1.0 + value * (1.0 - sigma)))).astype(low)
        pre[at, :] = low_grad
        wider = low_grad.astype(f32)
        return total + ((wider[0:8] + wider[8:16]) + (wider[16:24] + wider[24:32]))

    bias_part = lax.fori_loop(0, TR, through, jnp.zeros((8, C), f32), unroll=4)
    for child in range(4):
        lanes = slice(child * C, child * C + C)
        pack(child * C, jnp.dot(rows_t[lanes, :], pre[...], preferred_element_type=f32))
    size = group * rows
    for side in range(2):
        if size > 4 * C:
            packed[side, 4 * C : size, :] = jnp.zeros((size - 4 * C, 128), low)

    def plane_peer(step):
        index = lax.rem(mine + step, n_plane)
        return index, (index // 2 * 2 + core, line * 2 + lax.rem(index, 2))

    def line_peer(step):
        index = lax.rem(line + step, n_line)
        return index, (tm, index * 2 + lax.rem(pix, 2))

    def total_stages(base, rows, plane_in, line_out, line_in, sems):
        core_sems, plane_sems, line_sems, line_back, plane_back, pair_back = sems
        span = n_line * rows
        order = list(range(1, n_plane)) + [0]

        def span_of(step):
            return pl.ds(pl.multiple_of(base + plane_peer(step)[0] * span, 16), span)

        def swap(step):
            return pltpu.make_async_remote_copy(
                packed.at[1 - core, span_of(step)], core_in.at[span_of(step)],
                core_sems.at[0, step], core_sems.at[1, step], partner, MESH
            )

        def to_plane(step):
            return pltpu.make_async_remote_copy(
                half.at[span_of(step)], plane_in.at[step],
                plane_sems.at[0, step], plane_sems.at[1, step], plane_peer(step)[1], MESH
            )

        def to_line(step):
            index, device = line_peer(step)
            return pltpu.make_async_remote_copy(
                line_out.at[index], line_in.at[step],
                line_sems.at[0, step], line_sems.at[1, step], device, MESH
            )

        own = full.at[core, pl.ds(pl.multiple_of(base + (mine * n_line + line) * rows, 16), rows)]

        def place(step):
            index = lax.rem(mine + n_plane - step, n_plane)
            return full.at[core, pl.ds(pl.multiple_of(base + index * span, 16), span)]

        def back_line(step):
            return pltpu.make_async_remote_copy(
                own, own, line_back.at[0, step], line_back.at[1, step], line_peer(step)[1], MESH
            )

        def back_plane(step):
            return pltpu.make_async_remote_copy(
                place(0), place(0),
                plane_back.at[0, step], plane_back.at[1, step], plane_peer(step)[1], MESH
            )

        def back_pair(step):
            return pltpu.make_async_remote_copy(
                place(step), place(step),
                pair_back.at[0, step], pair_back.at[1, step], partner, MESH
            )

        def start():
            for step in order:
                swap(step).start()

        def enter_plane():
            for step in order:
                swap(step).wait()
                at = span_of(step)
                half[at, :] = (packed[core, at, :].astype(f32) + core_in[at, :].astype(f32)).astype(
                    low
                )
                if step:
                    to_plane(step).start()

        def enter_line():
            for step in range(1, n_plane):
                to_plane(step).wait()

            def line_sum(step):
                index, _ = line_peer(step)
                at = pl.ds(pl.multiple_of(base + mine * span + index * rows, 16), rows)
                total = half[at, :].astype(f32)
                for other in range(1, n_plane):
                    total = total + plane_in[
                        other, pl.ds(pl.multiple_of(index * rows, 16), rows), :
                    ].astype(f32)
                line_out[index] = total.astype(low)

            @pl.loop(1, n_line)
            def _(step):
                line_sum(step)
                to_line(step).start()

            line_sum(0)

        def turn():
            @pl.loop(1, n_line)
            def _(step):
                to_line(step).wait()

            def add(step, total):
                return total + line_in[step].astype(f32)

            first = pl.ds(pl.multiple_of(base + (mine * n_line + line) * rows, 16), rows)
            full[core, first, :] = lax.fori_loop(
                1, n_line, add, line_out[line].astype(f32)
            ).astype(low)

            @pl.loop(1, n_line)
            def _(step):
                back_line(step).start()

        def leave_line():
            @pl.loop(1, n_line)
            def _(step):
                back_line(step).wait()

            for step in range(1, n_plane):
                back_plane(step).start()
            back_pair(0).start()

        def leave_plane():
            for step in range(1, n_plane):
                back_plane(step).wait()
                back_pair(step).start()

        def finish():
            for step in range(n_plane):
                back_pair(step).wait()

        return start, enter_plane, enter_line, turn, leave_line, leave_plane, finish

    down = total_stages(0, rows, plane_in, line_out, line_in, total_sems[:6])
    rest = total_stages(
        size, rest_rows, rest_plane_in, rest_line_out, rest_line_in, total_sems[6:]
    )
    down[0]()

    for copy in forward:
        copy.wait()
    for side in range(2):
        edge[side] = jnp.dot(
            perm[side].astype(low), edge_recv[side], preferred_element_type=f32
        )
    for r in range(TR):
        wide[0, r + 1, 0:1, :] = edge[0, r : r + 1]
        wide[2, r + 1, TC - 1 : TC, :] = edge[1, r : r + 1]
    down[1]()

    def conv(r, sums):
        total = jnp.zeros((TC, C), f32)
        here = gwide[1, r + 1]
        new = []
        for a in range(3):
            for b in range(3):
                cells = wide[b, r + a]
                total = total + taps[3 * a + b : 3 * a + b + 1] * cells
                product = here * cells
                new.append(
                    sums[3 * a + b]
                    + ((product[0:8] + product[8:16]) + (product[16:24] + product[24:32]))
                )
        spread[pl.ds(pl.multiple_of(r * TC, TC), TC), :] = total.astype(low)
        return tuple(new)

    sums = lax.fori_loop(0, TR, conv, tuple(jnp.zeros((8, C), f32) for _ in range(9)))
    small = [jnp.sum(x, axis=0, keepdims=True) for x in sums]

    @pl.loop(0, n_tm)
    def _(i):
        at = pl.ds(pl.multiple_of(i * quarter, quarter), quarter)
        value = jnp.dot(spread[at, :], point[...], preferred_element_type=f32)
        mix_send[i] = (pooled[at, :].astype(f32) + value).astype(low)
        mixed_low[at, :] = mg_recv[i]

    for step in range(1, n_tm):
        exchange(mix_send, mix_recv, mix_sems, step).start()
    mix_recv[tm] = mix_send[tm]
    down[2]()

    across_rows = (((0,), (0,)), ((), ()))
    pack(size, lax.dot_general(spread[...], mixed_low[...], across_rows, preferred_element_type=f32))
    down[3]()

    for step in range(1, n_tm):
        exchange(mix_send, mix_recv, mix_sems, step).wait()

    def mixing(i, sums):
        at = pl.ds(pl.multiple_of(i * 16, 16), 16)
        cots = [cot[f, at, :].astype(f32) for f in range(n_tm)]
        mixes = [mix_recv[g, at, :].astype(f32) for g in range(n_tm)]
        new = []
        for f in range(n_tm):
            for g in range(n_tm):
                product = cots[f] * mixes[g]
                new.append(sums[n_tm * f + g] + (product[0:8] + product[8:16]))
        return tuple(new)

    sums = lax.fori_loop(
        0, quarter // 16, mixing, tuple(jnp.zeros((8, C), f32) for _ in range(n_tm * n_tm))
    )
    small += [jnp.sum(x, axis=0, keepdims=True) for x in sums]
    small.append(jnp.sum(bias_part, axis=0, keepdims=True))
    small.append(jnp.zeros((6, C), f32))
    pack(size + C, jnp.concatenate(small, axis=0))
    for side in range(2):
        packed[side, size + C + 32 :, :] = jnp.zeros((group * rest_rows - C - 32, 128), low)
    rest[0]()
    down[4]()

    for child in range(4):
        lanes = slice(child * C, child * C + C)
        value = lax.dot_general(
            pre[...], weight[lanes, :], (((1,), (1,)), ((), ())), preferred_element_type=f32
        )
        for side in range(2):
            fine[side, pl.ds(child, TR * TC, stride=4), :] = value[:, side * 128 : side * 128 + 128]
    rest[1]()

    @pl.loop(0, 2560 // 160)
    def _(i):
        at = pl.ds(pl.multiple_of(i * 160, 160), 160)
        for side in range(2):
            result[at, side * 128 : side * 128 + 128] = fine[side, at, :].astype(low)

    store = pltpu.make_async_copy(result, out_input, out_sems.at[0])
    store.start()
    rest[2]()
    down[5]()
    rest[3]()
    down[6]()
    store_down = pltpu.make_async_copy(
        full.at[:, 0:size], out_full.at[:, 0:size], out_sems.at[1]
    )
    store_down.start()
    for stage in rest[4:]:
        stage()
    store_rest = pltpu.make_async_copy(
        full.at[:, size:], out_full.at[:, size:], out_sems.at[2]
    )
    store_rest.start()
    store.wait()
    store_down.wait()
    store_rest.wait()


def unpack_kernel(
    scale, size, fine_in, full_in, out_input, out_down, out_bias, out_taps, out_point, out_mix,
    fine, full, down, bias, taps, point, mix, sems,
):
    f32 = jnp.float32
    through = pltpu.make_async_copy(fine_in, fine, sems.at[7])
    through.start()
    load = pltpu.make_async_copy(full_in, full, sems.at[1])
    load.start()
    through.wait()
    through = pltpu.make_async_copy(fine, out_input, sems.at[0])
    through.start()
    load.wait()
    for side in range(2):
        lanes = slice(side * 128, side * 128 + 128)
        tail = full[side, size + C : size + C + 32, :].astype(f32) * scale
        taps[:, lanes] = tail[0:9]
        for frame in range(mix.shape[0]):
            first = 9 + frame * mix.shape[1]
            mix[frame, :, lanes] = tail[first : first + mix.shape[1]]
        bias[lanes] = tail[25]
        point[:, lanes] = full[side, size : size + C, :].astype(f32) * scale
        down[:, lanes] = full[side, 0 : 4 * C, :].astype(f32) * scale
    stores = [
        pltpu.make_async_copy(here, there, sems.at[2 + i])
        for i, (here, there) in enumerate(
            [(down, out_down), (bias, out_bias), (taps, out_taps), (point, out_point), (mix, out_mix)]
        )
    ]
    for store in stores:
        store.start()
    for store in stores:
        store.wait()
    through.wait()


def on_device(
    activations, down_weight, down_bias, taps, point_weight, time_mix, edge_rows, cotangent
):
    frames = lax.axis_size("tm")
    tiles = lax.axis_size("pix")
    pixels = TR * TC
    quarter = pixels // frames
    scale = 1.0 / math.sqrt(frames * tiles * pixels)
    group = frames // 2 * tiles
    rows = -(-4 * C // (16 * group)) * 16
    rest_rows = -(-(C + 32) // (16 * group)) * 16
    size = group * (rows + rest_rows)
    f32, low = jnp.float32, jnp.bfloat16
    both = lambda n: pltpu.SemaphoreType.DMA((2, n))
    n_plane, n_line = frames // 2 * 2, tiles // 2
    hbm = pl.BlockSpec(memory_space=pltpu.HBM)
    fine, full = pl.pallas_call(
        functools.partial(kernel, rows, rest_rows),
        out_shape=[
            jax.ShapeDtypeStruct((4 * pixels, C), low),
            jax.ShapeDtypeStruct((2, size, 128), low),
        ],
        in_specs=[hbm] * 8,
        out_specs=[hbm] * 2,
        scratch_shapes=[
            pltpu.VMEM((4 * pixels, C), low),
            pltpu.VMEM((4 * C, C), low),
            pltpu.VMEM((1, C), f32),
            pltpu.VMEM((9, C), f32),
            pltpu.VMEM((C, C), low),
            pltpu.VMEM((frames, frames, C), f32),
            pltpu.VMEM((1, 2, TR), jnp.int32),
            pltpu.VMEM((frames, quarter, C), low),
            pltpu.VMEM((2, 32, 32), f32),
            pltpu.VMEM((4 * pixels, C), low),
            pltpu.VMEM((2, 4 * pixels, 128), f32),
            pltpu.VMEM((pixels, 4 * C), low),
            pltpu.VMEM((4 * C, pixels), low),
            pltpu.VMEM((pixels, C), f32),
            pltpu.VMEM((pixels, C), low),
            pltpu.VMEM((3, TR + 2, TC, C), f32),
            pltpu.VMEM((3, TR + 2, TC, C), f32),
            pltpu.VMEM((pixels, C), f32),
            pltpu.VMEM((pixels, C), low),
            pltpu.VMEM((pixels, C), low),
            pltpu.VMEM((frames, quarter, C), low),
            pltpu.VMEM((frames, quarter, C), low),
            pltpu.VMEM((frames, quarter, C), low),
            pltpu.VMEM((frames, quarter, C), low),
            pltpu.VMEM((2, 32, C), f32),
            pltpu.VMEM((2, 32, C), low),
            pltpu.VMEM((2, 32, C), low),
            pltpu.VMEM((2, 32, C), low),
            pltpu.VMEM((2, 32, C), low),
            pltpu.VMEM((pixels, C), low),
            pltpu.VMEM((2, size, 128), low),
            pltpu.VMEM((size, 128), low),
            pltpu.VMEM((size, 128), low),
            pltpu.VMEM((2, size, 128), low),
            pltpu.VMEM((n_plane, n_line * rows, 128), low),
            pltpu.VMEM((n_line, rows, 128), low),
            pltpu.VMEM((n_line, rows, 128), low),
            pltpu.VMEM((n_plane, n_line * rest_rows, 128), low),
            pltpu.VMEM((n_line, rest_rows, 128), low),
            pltpu.VMEM((n_line, rest_rows, 128), low),
            pltpu.SemaphoreType.DMA((8,)),
            pltpu.SemaphoreType.DMA((3,)),
            both(frames), both(frames), both(2), both(2),
        ]
        + 2 * [both(n_plane), both(n_plane), both(n_line), both(n_line), both(n_plane), both(n_plane)],
        compiler_params=pltpu.CompilerParams(
            collective_id=0, has_side_effects=True, vmem_limit_bytes=64 * 1024 * 1024
        ),
    )(
        activations.reshape(4 * pixels, C),
        down_weight,
        down_bias.reshape(1, C),
        taps,
        point_weight,
        time_mix,
        edge_rows,
        cotangent,
    )
    shapes = [(4 * C, C), (C,), (9, C), (C, C), (frames, frames, C)]
    outs = pl.pallas_call(
        functools.partial(unpack_kernel, scale, group * rows),
        out_shape=[jax.ShapeDtypeStruct((4 * pixels, C), low)]
        + [jax.ShapeDtypeStruct(shape, f32) for shape in shapes],
        in_specs=[hbm] * 2,
        out_specs=[hbm] * 6,
        scratch_shapes=[pltpu.VMEM((4 * pixels, C), low), pltpu.VMEM((2, size, 128), low)]
        + [pltpu.VMEM(shape, f32) for shape in shapes]
        + [pltpu.SemaphoreType.DMA((8,))],
        compiler_params=pltpu.CompilerParams(vmem_limit_bytes=64 * 1024 * 1024),
    )(fine, full)
    return (outs[0].reshape(1, 4 * pixels, C), *outs[1:])


def solution(mesh):
    in_specs = (
        P("tm", "pix", None),
        P(),
        P(),
        P(),
        P(),
        P(),
        P("pix", None, None),
        P(None, ("pix", "tm"), None),
    )
    out_specs = (P("tm", "pix", None), P(), P(), P(), P(), P())
    return jax.shard_map(
        on_device, mesh=mesh, in_specs=in_specs, out_specs=out_specs, check_vma=False
    )
```

```python
import functools
import math

import jax
import jax.numpy as jnp
from jax import lax
from jax.experimental import pallas as pl
from jax.experimental.pallas import tpu as pltpu
from jax.sharding import PartitionSpec as P

C = 256
TR = 20
TC = 32
MESH = pl.DeviceIdType.MESH


def kernel(
    rows, act_in, weight_in, bias_in, taps_in, point_in, mix_in, maps_in, cot_in,
    out_input, out_full,
    act, weight, bias, taps, point, mix, maps, cot, perm, result,
    fine, rows_in, rows_t, preact, pooled, wide, gwide, grad, spread, mixed_low,
    mg_send, mg_recv, mix_send, mix_recv, edge, edge_send, edge_recv, back_send, back_recv, pre,
    packed, core_in, half, plane_in, line_out, line_in, full,
    in_sems, out_sems, mg_sems, mix_sems, edge_sems, back_sems,
    core_sems, plane_sems, line_sems, line_back, plane_back, pair_back,
):
    f32, low = jnp.float32, jnp.bfloat16
    tm, pix = lax.axis_index("tm"), lax.axis_index("pix")
    n_tm, n_pix = lax.axis_size("tm"), lax.axis_size("pix")
    group = n_tm // 2 * n_pix
    core = lax.rem(tm, 2)
    me = tm // 2 * n_pix + pix
    n_plane, n_line = n_tm // 2 * 2, n_pix // 2
    mine, line = tm // 2 * 2 + lax.rem(pix, 2), pix // 2
    partner = (tm + 1 - 2 * core, pix)
    west, east = (tm, lax.rem(pix + n_pix - 1, n_pix)), (tm, lax.rem(pix + 1, n_pix))
    quarter = TR * TC // n_tm

    def peer(step):
        index = lax.rem(me + step, group)
        return index, (index // n_pix * 2 + core, lax.rem(index, n_pix))

    loads = [
        pltpu.make_async_copy(there, here, in_sems.at[i])
        for i, (there, here) in enumerate(
            [
                (cot_in, cot), (mix_in, mix), (act_in, act), (weight_in, weight), (bias_in, bias),
                (point_in, point), (taps_in, taps), (maps_in, maps),
            ]
        )
    ]
    for load in loads:
        load.start()

    barrier = pltpu.get_barrier_semaphore()
    pl.semaphore_signal(barrier, inc=1, device_id=partner, device_id_type=MESH)
    across = (lax.rem(partner[0] + 2, n_tm), pix)
    pl.semaphore_signal(barrier, inc=1, device_id=across, device_id_type=MESH)

    @pl.loop(1, group)
    def _(step):
        _, device = peer(step)
        pl.semaphore_signal(barrier, inc=1, device_id=device, device_id_type=MESH)

    loads[0].wait()
    loads[1].wait()
    for frame in range(n_tm):
        total = mix[0, frame : frame + 1] * cot[0].astype(f32)
        for source in range(1, n_tm):
            total = total + mix[source, frame : frame + 1] * cot[source].astype(f32)
        mg_send[frame] = total.astype(low)
    pl.semaphore_wait(barrier, group + 1)

    def exchange(send, recv, sems, step):
        target = lax.rem(tm + step, n_tm)
        return pltpu.make_async_remote_copy(
            send.at[target], recv.at[tm], sems.at[0, step], sems.at[1, step], (target, pix), MESH
        )

    for step in range(1, n_tm):
        exchange(mg_send, mg_recv, mg_sems, step).start()
    mg_recv[tm] = mg_send[tm]

    for load in loads[2:]:
        load.wait()
    perm[...] = jnp.zeros(perm.shape, f32)
    for side in range(2):
        row = lax.broadcasted_iota(jnp.int32, (TR, TR), 0)
        perm[side, 0:TR, 0:TR] = jnp.where(maps[0, side : side + 1, :] == row, 1.0, 0.0)

    @pl.loop(0, 2560 // 160)
    def _(i):
        at = pl.ds(pl.multiple_of(i * 160, 160), 160)
        for side in range(2):
            fine[side, at, :] = act[at, side * 128 : side * 128 + 128].astype(f32)

    for child in range(4):
        for side in range(2):
            lanes = slice(child * C + side * 128, child * C + side * 128 + 128)
            rows_in[:, lanes] = fine[side, pl.ds(child, TR * TC, stride=4), :].astype(low)

    @pl.loop(0, 4)
    def _(i):
        at = pl.ds(pl.multiple_of(i * 160, 160), 160)
        value = jnp.dot(rows_in[at, :], weight[...], preferred_element_type=f32) + bias[...]
        preact[at, :] = value
        pooled[at, :] = (value / (1.0 + jnp.exp(-value))).astype(low)

    def shifted(ref, values, r):
        ref[1, r + 1] = values
        ref[0, r + 1, 1:TC, :] = values[0 : TC - 1]
        ref[2, r + 1, 0 : TC - 1, :] = values[1:TC]

    for side in range(3):
        for r in (0, TR + 1):
            wide[side, r] = jnp.zeros((TC, C), f32)
            gwide[side, r] = jnp.zeros((TC, C), f32)

    @pl.loop(0, TR)
    def _(r):
        shifted(wide, pooled[pl.ds(pl.multiple_of(r * TC, TC), TC), :].astype(f32), r)

    edge[...] = jnp.zeros(edge.shape, f32)
    for r in range(TR):
        edge[0, r : r + 1] = wide[1, r + 1, 0:1, :]
        edge[1, r : r + 1] = wide[1, r + 1, TC - 1 : TC, :]
    edge_send[...] = edge[...].astype(low)

    def swap_edges(send, recv, sems):
        return [
            pltpu.make_async_remote_copy(
                send.at[0], recv.at[1], sems.at[0, 0], sems.at[1, 0], west, MESH
            ),
            pltpu.make_async_remote_copy(
                send.at[1], recv.at[0], sems.at[0, 1], sems.at[1, 1], east, MESH
            ),
        ]

    forward = swap_edges(edge_send, edge_recv, edge_sems)
    for copy in forward:
        copy.start()

    for child in range(4):
        lanes = slice(child * C, child * C + C)
        rows_t[lanes, :] = rows_in[:, lanes].T

    for step in range(1, n_tm):
        exchange(mg_send, mg_recv, mg_sems, step).wait()

    @pl.loop(0, n_tm)
    def _(i):
        value = lax.dot_general(
            mg_recv[i], point[...], (((1,), (1,)), ((), ())), preferred_element_type=f32
        )
        pre[pl.ds(pl.multiple_of(i * quarter, quarter), quarter), :] = value.astype(low)

    @pl.loop(0, TR)
    def _(r):
        shifted(gwide, pre[pl.ds(pl.multiple_of(r * TC, TC), TC), :].astype(f32), r)
        gwide[0, r + 1, 0:1, :] = jnp.zeros((1, C), f32)
        gwide[2, r + 1, TC - 1 : TC, :] = jnp.zeros((1, C), f32)

    edge[...] = jnp.zeros(edge.shape, f32)
    for r in range(TR):
        edge[0, r + 1 : r + 2] = gwide[1, r + 1, 0:1, :]
        edge[1, r + 1 : r + 2] = gwide[1, r + 1, TC - 1 : TC, :]
    for side in range(2):
        total = jnp.zeros((TR, C), f32)
        for a in range(3):
            tap = 3 * a + 2 * side
            total = total + taps[tap : tap + 1] * edge[side, 2 - a : 2 - a + TR]
        total = jnp.concatenate([total, jnp.zeros((32 - TR, C), f32)], axis=0).astype(low)
        back_send[side] = jnp.dot(perm[side].astype(low), total, preferred_element_type=f32).astype(low)
    backward = swap_edges(back_send, back_recv, back_sems)
    for copy in backward:
        copy.start()

    for copy in forward:
        copy.wait()
    for side in range(2):
        edge[side] = jnp.dot(perm[side].astype(low), edge_recv[side], preferred_element_type=f32)
    for r in range(TR):
        wide[0, r + 1, 0:1, :] = edge[0, r : r + 1]
        wide[2, r + 1, TC - 1 : TC, :] = edge[1, r : r + 1]

    def conv(r, sums):
        total = jnp.zeros((TC, C), f32)
        inner = mg_recv[r // (TR // n_tm), pl.ds(
            pl.multiple_of(lax.rem(r, TR // n_tm) * TC, TC), TC
        ), :].astype(f32)
        here = gwide[1, r + 1]
        new = []
        for a in range(3):
            for b in range(3):
                tap = taps[3 * a + b : 3 * a + b + 1]
                cells = wide[b, r + a]
                total = total + tap * cells
                inner = inner + tap * gwide[2 - b, r + 2 - a]
                product = here * cells
                new.append(
                    sums[3 * a + b]
                    + ((product[0:8] + product[8:16]) + (product[16:24] + product[24:32]))
                )
        at = pl.ds(pl.multiple_of(r * TC, TC), TC)
        spread[at, :] = total.astype(low)
        grad[at, :] = inner
        return tuple(new)

    sums = lax.fori_loop(0, TR, conv, tuple(jnp.zeros((8, C), f32) for _ in range(9)))
    taps_part = [jnp.sum(x, axis=0, keepdims=True) for x in sums]

    @pl.loop(0, n_tm)
    def _(i):
        at = pl.ds(pl.multiple_of(i * quarter, quarter), quarter)
        value = jnp.dot(spread[at, :], point[...], preferred_element_type=f32)
        mix_send[i] = (pooled[at, :].astype(f32) + value).astype(low)
        mixed_low[at, :] = mg_recv[i]

    for step in range(1, n_tm):
        exchange(mix_send, mix_recv, mix_sems, step).start()
    mix_recv[tm] = mix_send[tm]

    def pack(first, value):
        for side in range(2):
            packed[side, first : first + value.shape[0], :] = value[
                :, side * 128 : side * 128 + 128
            ].astype(low)

    across_rows = (((0,), (0,)), ((), ()))
    pack(4 * C, lax.dot_general(spread[...], mixed_low[...], across_rows, preferred_element_type=f32))

    for copy in backward:
        copy.wait()
    edge[...] = back_recv[...].astype(f32)
    for r in range(TR):
        grad[r * TC : r * TC + 1, :] += edge[0, r : r + 1]
        grad[r * TC + TC - 1 : r * TC + TC, :] += edge[1, r : r + 1]

    def through(r, total):
        at = pl.ds(pl.multiple_of(r * TC, TC), TC)
        value = preact[at, :]
        sigma = 1.0 / (1.0 + jnp.exp(-value))
        low_grad = (grad[at, :] * (sigma * (1.0 + value * (1.0 - sigma)))).astype(low)
        pre[at, :] = low_grad
        wider = low_grad.astype(f32)
        return total + ((wider[0:8] + wider[8:16]) + (wider[16:24] + wider[24:32]))

    span = n_line * rows

    def swap(block):
        at = pl.ds(pl.multiple_of(block * span, 16), span)
        return pltpu.make_async_remote_copy(
            packed.at[1 - core, at], core_in.at[at],
            core_sems.at[0, block], core_sems.at[1, block], partner, MESH
        )

    started = 0
    bias_part = lax.fori_loop(0, TR, through, jnp.zeros((8, C), f32), unroll=4)
    for child in range(4):
        lanes = slice(child * C, child * C + C)
        pack(child * C, jnp.dot(rows_t[lanes, :], pre[...], preferred_element_type=f32))
        ready = (child + 1) * C if child < 3 else 5 * C
        while started < n_plane and (started + 1) * span <= ready:
            swap(started).start()
            started += 1

    for step in range(1, n_tm):
        exchange(mix_send, mix_recv, mix_sems, step).wait()

    def mixing(i, sums):
        at = pl.ds(pl.multiple_of(i * 16, 16), 16)
        cots = [cot[f, at, :].astype(f32) for f in range(n_tm)]
        mixes = [mix_recv[g, at, :].astype(f32) for g in range(n_tm)]
        new = []
        for f in range(n_tm):
            for g in range(n_tm):
                product = cots[f] * mixes[g]
                new.append(sums[n_tm * f + g] + (product[0:8] + product[8:16]))
        return tuple(new)

    sums = lax.fori_loop(
        0, quarter // 16, mixing, tuple(jnp.zeros((8, C), f32) for _ in range(n_tm * n_tm))
    )
    small = taps_part + [jnp.sum(x, axis=0, keepdims=True) for x in sums]
    small.append(jnp.sum(bias_part, axis=0, keepdims=True))
    small.append(jnp.zeros((6, C), f32))
    pack(5 * C, jnp.concatenate(small, axis=0))
    for side in range(2):
        packed[side, 1312:, :] = jnp.zeros((group * rows - 1312, 128), low)

    def plane_peer(step):
        index = lax.rem(mine + step, n_plane)
        return index, (index // 2 * 2 + core, line * 2 + lax.rem(index, 2))

    def line_peer(step):
        index = lax.rem(line + step, n_line)
        return index, (tm, index * 2 + lax.rem(pix, 2))

    def span_of(step):
        index, _ = plane_peer(step)
        return pl.ds(pl.multiple_of(index * span, 16), span)

    def to_plane(step):
        return pltpu.make_async_remote_copy(
            half.at[span_of(step)], plane_in.at[step],
            plane_sems.at[0, step], plane_sems.at[1, step], plane_peer(step)[1], MESH
        )

    def to_line(step):
        index, device = line_peer(step)
        return pltpu.make_async_remote_copy(
            line_out.at[index], line_in.at[step],
            line_sems.at[0, step], line_sems.at[1, step], device, MESH
        )

    order = list(range(1, n_plane)) + [0]
    for block in range(started, n_plane):
        swap(block).start()
    for step in order:
        swap(plane_peer(step)[0]).wait()
        at = span_of(step)
        half[at, :] = (packed[core, at, :].astype(f32) + core_in[at, :].astype(f32)).astype(low)
        if step:
            to_plane(step).start()

    for child in range(4):
        lanes = slice(child * C, child * C + C)
        value = lax.dot_general(
            pre[...], weight[lanes, :], (((1,), (1,)), ((), ())), preferred_element_type=f32
        )
        for side in range(2):
            fine[side, pl.ds(child, TR * TC, stride=4), :] = value[:, side * 128 : side * 128 + 128]

    for step in range(1, n_plane):
        to_plane(step).wait()

    def line_sum(step):
        index, _ = line_peer(step)
        at = pl.ds(pl.multiple_of(mine * span + index * rows, 16), rows)
        total = half[at, :].astype(f32)
        for other in range(1, n_plane):
            total = total + plane_in[
                other, pl.ds(pl.multiple_of(index * rows, 16), rows), :
            ].astype(f32)
        line_out[index] = total.astype(low)

    @pl.loop(1, n_line)
    def _(step):
        line_sum(step)
        to_line(step).start()

    line_sum(0)

    @pl.loop(0, 2560 // 160)
    def _(i):
        at = pl.ds(pl.multiple_of(i * 160, 160), 160)
        for side in range(2):
            result[at, side * 128 : side * 128 + 128] = fine[side, at, :].astype(low)

    store = pltpu.make_async_copy(result, out_input, out_sems.at[0])
    store.start()

    @pl.loop(1, n_line)
    def _(step):
        to_line(step).wait()

    def add(step, total):
        return total + line_in[step].astype(f32)

    first = pl.ds(pl.multiple_of((mine * n_line + line) * rows, 16), rows)
    full[core, first, :] = lax.fori_loop(1, n_line, add, line_out[line].astype(f32)).astype(low)

    own = full.at[core, first]

    def place(step):
        index = lax.rem(mine + n_plane - step, n_plane)
        return full.at[core, pl.ds(pl.multiple_of(index * span, 16), span)]

    def back_line(step):
        return pltpu.make_async_remote_copy(
            own, own, line_back.at[0, step], line_back.at[1, step], line_peer(step)[1], MESH
        )

    def back_plane(step):
        return pltpu.make_async_remote_copy(
            place(0), place(0),
            plane_back.at[0, step], plane_back.at[1, step], plane_peer(step)[1], MESH
        )

    def back_pair(step):
        return pltpu.make_async_remote_copy(
            place(step), place(step),
            pair_back.at[0, step], pair_back.at[1, step], partner, MESH
        )

    @pl.loop(1, n_line)
    def _(step):
        back_line(step).start()

    @pl.loop(1, n_line)
    def _(step):
        back_line(step).wait()

    for step in range(1, n_plane):
        back_plane(step).start()
    back_pair(0).start()
    for step in range(1, n_plane):
        back_plane(step).wait()
        back_pair(step).start()
    for step in range(n_plane):
        back_pair(step).wait()

    store_full = pltpu.make_async_copy(full, out_full, out_sems.at[1])
    store_full.start()
    store.wait()
    store_full.wait()


def unpack_kernel(
    scale, fine_in, full_in, out_input, out_down, out_bias, out_taps, out_point, out_mix,
    fine, full, down, bias, taps, point, mix, sems,
):
    f32 = jnp.float32
    through = pltpu.make_async_copy(fine_in, fine, sems.at[7])
    through.start()
    load = pltpu.make_async_copy(full_in, full, sems.at[1])
    load.start()
    through.wait()
    through = pltpu.make_async_copy(fine, out_input, sems.at[0])
    through.start()
    load.wait()
    for side in range(2):
        lanes = slice(side * 128, side * 128 + 128)
        tail = full[side, 5 * C : 5 * C + 32, :].astype(f32) * scale
        taps[:, lanes] = tail[0:9]
        for frame in range(mix.shape[0]):
            first = 9 + frame * mix.shape[1]
            mix[frame, :, lanes] = tail[first : first + mix.shape[1]]
        bias[lanes] = tail[25]
        point[:, lanes] = full[side, 4 * C : 5 * C, :].astype(f32) * scale
        down[:, lanes] = full[side, 0 : 4 * C, :].astype(f32) * scale
    stores = [
        pltpu.make_async_copy(here, there, sems.at[2 + i])
        for i, (here, there) in enumerate(
            [(down, out_down), (bias, out_bias), (taps, out_taps), (point, out_point), (mix, out_mix)]
        )
    ]
    for store in stores:
        store.start()
    for store in stores:
        store.wait()
    through.wait()


def on_device(
    activations, down_weight, down_bias, taps, point_weight, time_mix, edge_rows, cotangent
):
    frames = lax.axis_size("tm")
    tiles = lax.axis_size("pix")
    pixels = TR * TC
    quarter = pixels // frames
    scale = 1.0 / math.sqrt(frames * tiles * pixels)
    group = frames // 2 * tiles
    rows = -(-1312 // (16 * group)) * 16
    f32, low = jnp.float32, jnp.bfloat16
    both = lambda n: pltpu.SemaphoreType.DMA((2, n))
    n_plane, n_line = frames // 2 * 2, tiles // 2
    hbm = pl.BlockSpec(memory_space=pltpu.HBM)
    fine, full = pl.pallas_call(
        functools.partial(kernel, rows),
        out_shape=[
            jax.ShapeDtypeStruct((4 * pixels, C), low),
            jax.ShapeDtypeStruct((2, group * rows, 128), low),
        ],
        in_specs=[hbm] * 8,
        out_specs=[hbm] * 2,
        scratch_shapes=[
            pltpu.VMEM((4 * pixels, C), low),
            pltpu.VMEM((4 * C, C), low),
            pltpu.VMEM((1, C), f32),
            pltpu.VMEM((9, C), f32),
            pltpu.VMEM((C, C), low),
            pltpu.VMEM((frames, frames, C), f32),
            pltpu.VMEM((1, 2, TR), jnp.int32),
            pltpu.VMEM((frames, quarter, C), low),
            pltpu.VMEM((2, 32, 32), f32),
            pltpu.VMEM((4 * pixels, C), low),
            pltpu.VMEM((2, 4 * pixels, 128), f32),
            pltpu.VMEM((pixels, 4 * C), low),
            pltpu.VMEM((4 * C, pixels), low),
            pltpu.VMEM((pixels, C), f32),
            pltpu.VMEM((pixels, C), low),
            pltpu.VMEM((3, TR + 2, TC, C), f32),
            pltpu.VMEM((3, TR + 2, TC, C), f32),
            pltpu.VMEM((pixels, C), f32),
            pltpu.VMEM((pixels, C), low),
            pltpu.VMEM((pixels, C), low),
            pltpu.VMEM((frames, quarter, C), low),
            pltpu.VMEM((frames, quarter, C), low),
            pltpu.VMEM((frames, quarter, C), low),
            pltpu.VMEM((frames, quarter, C), low),
            pltpu.VMEM((2, 32, C), f32),
            pltpu.VMEM((2, 32, C), low),
            pltpu.VMEM((2, 32, C), low),
            pltpu.VMEM((2, 32, C), low),
            pltpu.VMEM((2, 32, C), low),
            pltpu.VMEM((pixels, C), low),
            pltpu.VMEM((2, group * rows, 128), low),
            pltpu.VMEM((group * rows, 128), low),
            pltpu.VMEM((group * rows, 128), low),
            pltpu.VMEM((n_plane, n_line * rows, 128), low),
            pltpu.VMEM((n_line, rows, 128), low),
            pltpu.VMEM((n_line, rows, 128), low),
            pltpu.VMEM((2, group * rows, 128), low),
            pltpu.SemaphoreType.DMA((8,)),
            pltpu.SemaphoreType.DMA((2,)),
            both(frames), both(frames), both(2), both(2),
            both(n_plane), both(n_plane), both(n_line), both(n_line), both(n_plane), both(n_plane),
        ],
        compiler_params=pltpu.CompilerParams(
            collective_id=0, has_side_effects=True, vmem_limit_bytes=64 * 1024 * 1024
        ),
    )(
        activations.reshape(4 * pixels, C),
        down_weight,
        down_bias.reshape(1, C),
        taps,
        point_weight,
        time_mix,
        edge_rows,
        cotangent,
    )
    shapes = [(4 * C, C), (C,), (9, C), (C, C), (frames, frames, C)]
    outs = pl.pallas_call(
        functools.partial(unpack_kernel, scale),
        out_shape=[jax.ShapeDtypeStruct((4 * pixels, C), low)]
        + [jax.ShapeDtypeStruct(shape, f32) for shape in shapes],
        in_specs=[hbm] * 2,
        out_specs=[hbm] * 6,
        scratch_shapes=[pltpu.VMEM((4 * pixels, C), low), pltpu.VMEM((2, group * rows, 128), low)]
        + [pltpu.VMEM(shape, f32) for shape in shapes]
        + [pltpu.SemaphoreType.DMA((8,))],
        compiler_params=pltpu.CompilerParams(vmem_limit_bytes=64 * 1024 * 1024),
    )(fine, full)
    return (outs[0].reshape(1, 4 * pixels, C), *outs[1:])


def solution(mesh):
    in_specs = (
        P("tm", "pix", None),
        P(),
        P(),
        P(),
        P(),
        P(),
        P("pix", None, None),
        P(None, ("pix", "tm"), None),
    )
    out_specs = (P("tm", "pix", None), P(), P(), P(), P(), P())
    return jax.shard_map(
        on_device, mesh=mesh, in_specs=in_specs, out_specs=out_specs, check_vma=False
    )
```

```python
import functools
import math

import jax
import jax.numpy as jnp
from jax import lax
from jax.experimental import pallas as pl
from jax.experimental.pallas import tpu as pltpu
from jax.sharding import PartitionSpec as P

C = 256
TR = 20
TC = 32
MESH = pl.DeviceIdType.MESH


def kernel(
    rows, act_in, weight_in, bias_in, taps_in, point_in, mix_in, maps_in, cot_in,
    out_input, out_full,
    act, weight, bias, taps, point, mix, maps, cot, perm, result,
    fine, rows_in, rows_t, preact, pooled, wide, gwide, grad, spread, mixed_low,
    mg_send, mg_recv, mix_send, mix_recv, edge, edge_send, edge_recv, back_send, back_recv, pre,
    packed, core_in, half, plane_in, line_out, line_in, full,
    in_sems, out_sems, mg_sems, mix_sems, edge_sems, back_sems,
    core_sems, plane_sems, line_sems, line_back, plane_back, pair_back,
):
    f32, low = jnp.float32, jnp.bfloat16
    tm, pix = lax.axis_index("tm"), lax.axis_index("pix")
    n_tm, n_pix = lax.axis_size("tm"), lax.axis_size("pix")
    group = n_tm // 2 * n_pix
    core = lax.rem(tm, 2)
    me = tm // 2 * n_pix + pix
    n_plane, n_line = n_tm // 2 * 2, n_pix // 2
    mine, line = tm // 2 * 2 + lax.rem(pix, 2), pix // 2
    partner = (tm + 1 - 2 * core, pix)
    west, east = (tm, lax.rem(pix + n_pix - 1, n_pix)), (tm, lax.rem(pix + 1, n_pix))
    quarter = TR * TC // n_tm

    def peer(step):
        index = lax.rem(me + step, group)
        return index, (index // n_pix * 2 + core, lax.rem(index, n_pix))

    loads = [
        pltpu.make_async_copy(there, here, in_sems.at[i])
        for i, (there, here) in enumerate(
            [
                (cot_in, cot), (mix_in, mix), (act_in, act), (weight_in, weight), (bias_in, bias),
                (point_in, point), (taps_in, taps), (maps_in, maps),
            ]
        )
    ]
    for load in loads:
        load.start()

    barrier = pltpu.get_barrier_semaphore()
    pl.semaphore_signal(barrier, inc=1, device_id=partner, device_id_type=MESH)
    across = (lax.rem(partner[0] + 2, n_tm), pix)
    pl.semaphore_signal(barrier, inc=1, device_id=across, device_id_type=MESH)

    @pl.loop(1, group)
    def _(step):
        _, device = peer(step)
        pl.semaphore_signal(barrier, inc=1, device_id=device, device_id_type=MESH)

    loads[0].wait()
    loads[1].wait()
    for frame in range(n_tm):
        total = mix[0, frame : frame + 1] * cot[0].astype(f32)
        for source in range(1, n_tm):
            total = total + mix[source, frame : frame + 1] * cot[source].astype(f32)
        mg_send[frame] = total.astype(low)
    pl.semaphore_wait(barrier, group + 1)

    def exchange(send, recv, sems, step):
        target = lax.rem(tm + step, n_tm)
        return pltpu.make_async_remote_copy(
            send.at[target], recv.at[tm], sems.at[0, step], sems.at[1, step], (target, pix), MESH
        )

    for step in range(1, n_tm):
        exchange(mg_send, mg_recv, mg_sems, step).start()
    mg_recv[tm] = mg_send[tm]

    for load in loads[2:]:
        load.wait()
    perm[...] = jnp.zeros(perm.shape, f32)
    for side in range(2):
        row = lax.broadcasted_iota(jnp.int32, (TR, TR), 0)
        perm[side, 0:TR, 0:TR] = jnp.where(maps[0, side : side + 1, :] == row, 1.0, 0.0)

    @pl.loop(0, 2560 // 160, unroll=4)
    def _(i):
        at = pl.ds(pl.multiple_of(i * 160, 160), 160)
        for side in range(2):
            fine[side, at, :] = act[at, side * 128 : side * 128 + 128].astype(f32)

    for child in range(4):
        for side in range(2):
            lanes = slice(child * C + side * 128, child * C + side * 128 + 128)
            rows_in[:, lanes] = fine[side, pl.ds(child, TR * TC, stride=4), :].astype(low)

    @pl.loop(0, 4)
    def _(i):
        at = pl.ds(pl.multiple_of(i * 160, 160), 160)
        value = jnp.dot(rows_in[at, :], weight[...], preferred_element_type=f32) + bias[...]
        preact[at, :] = value
        pooled[at, :] = (value / (1.0 + jnp.exp(-value))).astype(low)

    def shifted(ref, values, r):
        ref[1, r + 1] = values
        ref[0, r + 1, 1:TC, :] = values[0 : TC - 1]
        ref[2, r + 1, 0 : TC - 1, :] = values[1:TC]

    for side in range(3):
        for r in (0, TR + 1):
            wide[side, r] = jnp.zeros((TC, C), f32)
            gwide[side, r] = jnp.zeros((TC, C), f32)

    @pl.loop(0, TR)
    def _(r):
        shifted(wide, pooled[pl.ds(pl.multiple_of(r * TC, TC), TC), :].astype(f32), r)

    edge[...] = jnp.zeros(edge.shape, f32)
    for r in range(TR):
        edge[0, r : r + 1] = wide[1, r + 1, 0:1, :]
        edge[1, r : r + 1] = wide[1, r + 1, TC - 1 : TC, :]
    edge_send[...] = edge[...].astype(low)

    def swap_edges(send, recv, sems):
        return [
            pltpu.make_async_remote_copy(
                send.at[0], recv.at[1], sems.at[0, 0], sems.at[1, 0], west, MESH
            ),
            pltpu.make_async_remote_copy(
                send.at[1], recv.at[0], sems.at[0, 1], sems.at[1, 1], east, MESH
            ),
        ]

    forward = swap_edges(edge_send, edge_recv, edge_sems)
    for copy in forward:
        copy.start()

    for child in range(4):
        lanes = slice(child * C, child * C + C)
        rows_t[lanes, :] = rows_in[:, lanes].T

    for step in range(1, n_tm):
        exchange(mg_send, mg_recv, mg_sems, step).wait()

    @pl.loop(0, n_tm)
    def _(i):
        value = lax.dot_general(
            mg_recv[i], point[...], (((1,), (1,)), ((), ())), preferred_element_type=f32
        )
        pre[pl.ds(pl.multiple_of(i * quarter, quarter), quarter), :] = value.astype(low)

    @pl.loop(0, TR)
    def _(r):
        shifted(gwide, pre[pl.ds(pl.multiple_of(r * TC, TC), TC), :].astype(f32), r)
        gwide[0, r + 1, 0:1, :] = jnp.zeros((1, C), f32)
        gwide[2, r + 1, TC - 1 : TC, :] = jnp.zeros((1, C), f32)

    edge[...] = jnp.zeros(edge.shape, f32)
    for r in range(TR):
        edge[0, r + 1 : r + 2] = gwide[1, r + 1, 0:1, :]
        edge[1, r + 1 : r + 2] = gwide[1, r + 1, TC - 1 : TC, :]
    for side in range(2):
        total = jnp.zeros((TR, C), f32)
        for a in range(3):
            tap = 3 * a + 2 * side
            total = total + taps[tap : tap + 1] * edge[side, 2 - a : 2 - a + TR]
        total = jnp.concatenate([total, jnp.zeros((32 - TR, C), f32)], axis=0).astype(low)
        back_send[side] = jnp.dot(perm[side].astype(low), total, preferred_element_type=f32).astype(low)
    backward = swap_edges(back_send, back_recv, back_sems)
    for copy in backward:
        copy.start()

    for copy in forward:
        copy.wait()
    for side in range(2):
        edge[side] = jnp.dot(perm[side].astype(low), edge_recv[side], preferred_element_type=f32)
    for r in range(TR):
        wide[0, r + 1, 0:1, :] = edge[0, r : r + 1]
        wide[2, r + 1, TC - 1 : TC, :] = edge[1, r : r + 1]

    def conv(r, sums):
        total = jnp.zeros((TC, C), f32)
        inner = mg_recv[r // (TR // n_tm), pl.ds(
            pl.multiple_of(lax.rem(r, TR // n_tm) * TC, TC), TC
        ), :].astype(f32)
        here = gwide[1, r + 1]
        new = []
        for a in range(3):
            for b in range(3):
                tap = taps[3 * a + b : 3 * a + b + 1]
                cells = wide[b, r + a]
                total = total + tap * cells
                inner = inner + tap * gwide[2 - b, r + 2 - a]
                product = here * cells
                new.append(
                    sums[3 * a + b]
                    + ((product[0:8] + product[8:16]) + (product[16:24] + product[24:32]))
                )
        at = pl.ds(pl.multiple_of(r * TC, TC), TC)
        spread[at, :] = total.astype(low)
        grad[at, :] = inner
        return tuple(new)

    sums = lax.fori_loop(0, TR, conv, tuple(jnp.zeros((8, C), f32) for _ in range(9)), unroll=2)
    taps_part = [jnp.sum(x, axis=0, keepdims=True) for x in sums]

    @pl.loop(0, n_tm)
    def _(i):
        at = pl.ds(pl.multiple_of(i * quarter, quarter), quarter)
        value = jnp.dot(spread[at, :], point[...], preferred_element_type=f32)
        mix_send[i] = (pooled[at, :].astype(f32) + value).astype(low)
        mixed_low[at, :] = mg_recv[i]

    for step in range(1, n_tm):
        exchange(mix_send, mix_recv, mix_sems, step).start()
    mix_recv[tm] = mix_send[tm]

    def pack(first, value):
        for side in range(2):
            packed[side, first : first + value.shape[0], :] = value[
                :, side * 128 : side * 128 + 128
            ].astype(low)

    across_rows = (((0,), (0,)), ((), ()))
    pack(4 * C, lax.dot_general(spread[...], mixed_low[...], across_rows, preferred_element_type=f32))

    for copy in backward:
        copy.wait()
    edge[...] = back_recv[...].astype(f32)
    for r in range(TR):
        grad[r * TC : r * TC + 1, :] += edge[0, r : r + 1]
        grad[r * TC + TC - 1 : r * TC + TC, :] += edge[1, r : r + 1]

    def through(r, total):
        at = pl.ds(pl.multiple_of(r * TC, TC), TC)
        value = preact[at, :]
        sigma = 1.0 / (1.0 + jnp.exp(-value))
        low_grad = (grad[at, :] * (sigma * (1.0 + value * (1.0 - sigma)))).astype(low)
        pre[at, :] = low_grad
        wider = low_grad.astype(f32)
        return total + ((wider[0:8] + wider[8:16]) + (wider[16:24] + wider[24:32]))

    span = n_line * rows

    def swap(block):
        at = pl.ds(pl.multiple_of(block * span, 16), span)
        return pltpu.make_async_remote_copy(
            packed.at[1 - core, at], core_in.at[at],
            core_sems.at[0, block], core_sems.at[1, block], partner, MESH
        )

    started = 0
    bias_part = lax.fori_loop(0, TR, through, jnp.zeros((8, C), f32), unroll=4)
    for child in range(4):
        lanes = slice(child * C, child * C + C)
        pack(child * C, jnp.dot(rows_t[lanes, :], pre[...], preferred_element_type=f32))
        ready = (child + 1) * C if child < 3 else 5 * C
        while started < n_plane and (started + 1) * span <= ready:
            swap(started).start()
            started += 1

    for step in range(1, n_tm):
        exchange(mix_send, mix_recv, mix_sems, step).wait()

    def mixing(i, sums):
        at = pl.ds(pl.multiple_of(i * 16, 16), 16)
        cots = [cot[f, at, :].astype(f32) for f in range(n_tm)]
        mixes = [mix_recv[g, at, :].astype(f32) for g in range(n_tm)]
        new = []
        for f in range(n_tm):
            for g in range(n_tm):
                product = cots[f] * mixes[g]
                new.append(sums[n_tm * f + g] + (product[0:8] + product[8:16]))
        return tuple(new)

    sums = lax.fori_loop(
        0, quarter // 16, mixing, tuple(jnp.zeros((8, C), f32) for _ in range(n_tm * n_tm))
    )
    small = taps_part + [jnp.sum(x, axis=0, keepdims=True) for x in sums]
    small.append(jnp.sum(bias_part, axis=0, keepdims=True))
    small.append(jnp.zeros((6, C), f32))
    pack(5 * C, jnp.concatenate(small, axis=0))
    for side in range(2):
        packed[side, 1312:, :] = jnp.zeros((group * rows - 1312, 128), low)

    def plane_peer(step):
        index = lax.rem(mine + step, n_plane)
        return index, (index // 2 * 2 + core, line * 2 + lax.rem(index, 2))

    def line_peer(step):
        index = lax.rem(line + step, n_line)
        return index, (tm, index * 2 + lax.rem(pix, 2))

    def span_of(step):
        index, _ = plane_peer(step)
        return pl.ds(pl.multiple_of(index * span, 16), span)

    def to_plane(step):
        return pltpu.make_async_remote_copy(
            half.at[span_of(step)], plane_in.at[step],
            plane_sems.at[0, step], plane_sems.at[1, step], plane_peer(step)[1], MESH
        )

    def to_line(step):
        index, device = line_peer(step)
        return pltpu.make_async_remote_copy(
            line_out.at[index], line_in.at[step],
            line_sems.at[0, step], line_sems.at[1, step], device, MESH
        )

    order = list(range(1, n_plane)) + [0]
    for block in range(started, n_plane):
        swap(block).start()
    for step in order:
        swap(plane_peer(step)[0]).wait()
        at = span_of(step)
        half[at, :] = (packed[core, at, :].astype(f32) + core_in[at, :].astype(f32)).astype(low)
        if step:
            to_plane(step).start()

    for child in range(4):
        lanes = slice(child * C, child * C + C)
        value = lax.dot_general(
            pre[...], weight[lanes, :], (((1,), (1,)), ((), ())), preferred_element_type=f32
        )
        for side in range(2):
            fine[side, pl.ds(child, TR * TC, stride=4), :] = value[:, side * 128 : side * 128 + 128]

    for step in range(1, n_plane):
        to_plane(step).wait()

    def line_sum(step):
        index, _ = line_peer(step)
        at = pl.ds(pl.multiple_of(mine * span + index * rows, 16), rows)
        total = half[at, :].astype(f32)
        for other in range(1, n_plane):
            total = total + plane_in[
                other, pl.ds(pl.multiple_of(index * rows, 16), rows), :
            ].astype(f32)
        line_out[index] = total.astype(low)

    @pl.loop(1, n_line)
    def _(step):
        line_sum(step)
        to_line(step).start()

    line_sum(0)

    @pl.loop(0, 2560 // 160, unroll=4)
    def _(i):
        at = pl.ds(pl.multiple_of(i * 160, 160), 160)
        for side in range(2):
            result[at, side * 128 : side * 128 + 128] = fine[side, at, :].astype(low)

    store = pltpu.make_async_copy(result, out_input, out_sems.at[0])
    store.start()

    @pl.loop(1, n_line)
    def _(step):
        to_line(step).wait()

    def add(step, total):
        return total + line_in[step].astype(f32)

    first = pl.ds(pl.multiple_of((mine * n_line + line) * rows, 16), rows)
    full[core, first, :] = lax.fori_loop(1, n_line, add, line_out[line].astype(f32)).astype(low)

    own = full.at[core, first]

    def place(step):
        index = lax.rem(mine + n_plane - step, n_plane)
        return full.at[core, pl.ds(pl.multiple_of(index * span, 16), span)]

    def back_line(step):
        return pltpu.make_async_remote_copy(
            own, own, line_back.at[0, step], line_back.at[1, step], line_peer(step)[1], MESH
        )

    def back_plane(step):
        return pltpu.make_async_remote_copy(
            place(0), place(0),
            plane_back.at[0, step], plane_back.at[1, step], plane_peer(step)[1], MESH
        )

    def back_pair(step):
        return pltpu.make_async_remote_copy(
            place(step), place(step),
            pair_back.at[0, step], pair_back.at[1, step], partner, MESH
        )

    @pl.loop(1, n_line)
    def _(step):
        back_line(step).start()

    @pl.loop(1, n_line)
    def _(step):
        back_line(step).wait()

    for step in range(1, n_plane):
        back_plane(step).start()
    back_pair(0).start()
    for step in range(1, n_plane):
        back_plane(step).wait()
        back_pair(step).start()
    for step in range(n_plane):
        back_pair(step).wait()

    store_full = pltpu.make_async_copy(full, out_full, out_sems.at[1])
    store_full.start()
    store.wait()
    store_full.wait()


def unpack_kernel(
    scale, fine_in, full_in, out_input, out_down, out_bias, out_taps, out_point, out_mix,
    fine, full, down, bias, taps, point, mix, sems,
):
    f32 = jnp.float32
    through = pltpu.make_async_copy(fine_in, fine, sems.at[7])
    through.start()
    load = pltpu.make_async_copy(full_in, full, sems.at[1])
    load.start()
    through.wait()
    through = pltpu.make_async_copy(fine, out_input, sems.at[0])
    through.start()
    load.wait()
    for side in range(2):
        lanes = slice(side * 128, side * 128 + 128)
        tail = full[side, 5 * C : 5 * C + 32, :].astype(f32) * scale
        taps[:, lanes] = tail[0:9]
        for frame in range(mix.shape[0]):
            first = 9 + frame * mix.shape[1]
            mix[frame, :, lanes] = tail[first : first + mix.shape[1]]
        bias[lanes] = tail[25]
        point[:, lanes] = full[side, 4 * C : 5 * C, :].astype(f32) * scale
        down[:, lanes] = full[side, 0 : 4 * C, :].astype(f32) * scale
    stores = [
        pltpu.make_async_copy(here, there, sems.at[2 + i])
        for i, (here, there) in enumerate(
            [(down, out_down), (bias, out_bias), (taps, out_taps), (point, out_point), (mix, out_mix)]
        )
    ]
    for store in stores:
        store.start()
    for store in stores:
        store.wait()
    through.wait()


def on_device(
    activations, down_weight, down_bias, taps, point_weight, time_mix, edge_rows, cotangent
):
    frames = lax.axis_size("tm")
    tiles = lax.axis_size("pix")
    pixels = TR * TC
    quarter = pixels // frames
    scale = 1.0 / math.sqrt(frames * tiles * pixels)
    group = frames // 2 * tiles
    rows = -(-1312 // (16 * group)) * 16
    f32, low = jnp.float32, jnp.bfloat16
    both = lambda n: pltpu.SemaphoreType.DMA((2, n))
    n_plane, n_line = frames // 2 * 2, tiles // 2
    hbm = pl.BlockSpec(memory_space=pltpu.HBM)
    fine, full = pl.pallas_call(
        functools.partial(kernel, rows),
        out_shape=[
            jax.ShapeDtypeStruct((4 * pixels, C), low),
            jax.ShapeDtypeStruct((2, group * rows, 128), low),
        ],
        in_specs=[hbm] * 8,
        out_specs=[hbm] * 2,
        scratch_shapes=[
            pltpu.VMEM((4 * pixels, C), low),
            pltpu.VMEM((4 * C, C), low),
            pltpu.VMEM((1, C), f32),
            pltpu.VMEM((9, C), f32),
            pltpu.VMEM((C, C), low),
            pltpu.VMEM((frames, frames, C), f32),
            pltpu.VMEM((1, 2, TR), jnp.int32),
            pltpu.VMEM((frames, quarter, C), low),
            pltpu.VMEM((2, 32, 32), f32),
            pltpu.VMEM((4 * pixels, C), low),
            pltpu.VMEM((2, 4 * pixels, 128), f32),
            pltpu.VMEM((pixels, 4 * C), low),
            pltpu.VMEM((4 * C, pixels), low),
            pltpu.VMEM((pixels, C), f32),
            pltpu.VMEM((pixels, C), low),
            pltpu.VMEM((3, TR + 2, TC, C), f32),
            pltpu.VMEM((3, TR + 2, TC, C), f32),
            pltpu.VMEM((pixels, C), f32),
            pltpu.VMEM((pixels, C), low),
            pltpu.VMEM((pixels, C), low),
            pltpu.VMEM((frames, quarter, C), low),
            pltpu.VMEM((frames, quarter, C), low),
            pltpu.VMEM((frames, quarter, C), low),
            pltpu.VMEM((frames, quarter, C), low),
            pltpu.VMEM((2, 32, C), f32),
            pltpu.VMEM((2, 32, C), low),
            pltpu.VMEM((2, 32, C), low),
            pltpu.VMEM((2, 32, C), low),
            pltpu.VMEM((2, 32, C), low),
            pltpu.VMEM((pixels, C), low),
            pltpu.VMEM((2, group * rows, 128), low),
            pltpu.VMEM((group * rows, 128), low),
            pltpu.VMEM((group * rows, 128), low),
            pltpu.VMEM((n_plane, n_line * rows, 128), low),
            pltpu.VMEM((n_line, rows, 128), low),
            pltpu.VMEM((n_line, rows, 128), low),
            pltpu.VMEM((2, group * rows, 128), low),
            pltpu.SemaphoreType.DMA((8,)),
            pltpu.SemaphoreType.DMA((2,)),
            both(frames), both(frames), both(2), both(2),
            both(n_plane), both(n_plane), both(n_line), both(n_line), both(n_plane), both(n_plane),
        ],
        compiler_params=pltpu.CompilerParams(
            collective_id=0, has_side_effects=True, vmem_limit_bytes=64 * 1024 * 1024
        ),
    )(
        activations.reshape(4 * pixels, C),
        down_weight,
        down_bias.reshape(1, C),
        taps,
        point_weight,
        time_mix,
        edge_rows,
        cotangent,
    )
    shapes = [(4 * C, C), (C,), (9, C), (C, C), (frames, frames, C)]
    outs = pl.pallas_call(
        functools.partial(unpack_kernel, scale),
        out_shape=[jax.ShapeDtypeStruct((4 * pixels, C), low)]
        + [jax.ShapeDtypeStruct(shape, f32) for shape in shapes],
        in_specs=[hbm] * 2,
        out_specs=[hbm] * 6,
        scratch_shapes=[pltpu.VMEM((4 * pixels, C), low), pltpu.VMEM((2, group * rows, 128), low)]
        + [pltpu.VMEM(shape, f32) for shape in shapes]
        + [pltpu.SemaphoreType.DMA((8,))],
        compiler_params=pltpu.CompilerParams(vmem_limit_bytes=64 * 1024 * 1024),
    )(fine, full)
    return (outs[0].reshape(1, 4 * pixels, C), *outs[1:])


def solution(mesh):
    in_specs = (
        P("tm", "pix", None),
        P(),
        P(),
        P(),
        P(),
        P(),
        P("pix", None, None),
        P(None, ("pix", "tm"), None),
    )
    out_specs = (P("tm", "pix", None), P(), P(), P(), P(), P())
    return jax.shard_map(
        on_device, mesh=mesh, in_specs=in_specs, out_specs=out_specs, check_vma=False
    )
```
